256 devices in a mesh: ctx: 16 (over y_lo, x, core), tp: 16 (over y_hi, z).
Axes of the slice: x: 4, y: 4 (y_hi: 2, y_lo: 2; y = y_hi * 2 + y_lo), z: 8, core: 2. Of those that a mesh axis runs over, the one named last changes fastest.
Arguments:
- query: bfloat16 [4096, 32768], P('tp', 'ctx'), may hold values from -6 to 6
- key_in: bfloat16 [4096, 32768], P('tp', 'ctx'), may hold values from -6 to 6
- value: bfloat16 [4096, 32768], P('tp', 'ctx'), may hold values from -6 to 6
- grad_out: bfloat16 [4096, 32768], P('tp', 'ctx'), may hold values from -6 to 6
- filter_raw: float32 [256, 32768], P('ctx'), may hold values from -6 to 6
Outputs:
- grad_query: bfloat16 [4096, 32768], P('tp', 'ctx')
- grad_key: bfloat16 [4096, 32768], P('tp', 'ctx')
- grad_value: bfloat16 [4096, 32768], P('tp', 'ctx')
- filter_grad: float32 [256, 32768], P('ctx', 'tp')
The draws below stay inside these ranges and needn't reach their ends.
All inputs are finite; a program needn't handle non-finite values.
Results may differ from the reference program's by a relative error of at most 0.0058.
Values may be sent and summed in bfloat16 or wider, within the bound.
No kernel may reach another device: no remote copies, remote signals or barrier semaphores. Data moves between devices by JAX's collectives and lax.ppermute only.
A program may use at most 128 MiB of HBM per device.

```python
import math
import jax
import jax.numpy as jnp
from jax import lax

LEN = 32768
C = 4096
FILTERS = 256
N_TP = 16


def level_of(stream_key, shape, shards, low, largest):
    loudness, own = 1.0, jax.random.fold_in(stream_key, 6)
    for axis_at, shards_of in shards:
        draws = jnp.exp(jax.random.uniform(jax.random.fold_in(own, axis_at), (shards_of,), jnp.float32, low / len(shards), largest / len(shards)))
        loudness = loudness * jnp.repeat(draws, shape[axis_at] // shards_of).reshape([-1 if axis == axis_at else 1 for axis in range(len(shape))])
    return loudness


def centred(rng, shape, deviation, reach, cuts=(), dtype=jnp.bfloat16):
    drawn = deviation * jax.random.normal(rng, shape, jnp.float32)
    if cuts:
        drawn = drawn * level_of(rng, shape, cuts, -0.22, 0.18)
    return jnp.clip(drawn, -reach, reach).astype(dtype)


def setup_inputs(seed: int = 0) -> dict:
    arg_keys = jax.random.split(jax.random.key(seed), 6)
    return {
        "query": centred(arg_keys[0], (C, LEN), 1.0, 6.0, ((0, 16), (1, 16))),
        "key_in": centred(arg_keys[1], (C, LEN), 1.0, 6.0, ((0, 16), (1, 16))),
        "value": centred(arg_keys[2], (C, LEN), 1.0, 6.0, ((0, 16), (1, 16))),
        "grad_out": centred(arg_keys[3], (C, LEN), 1.0, 6.0, ((0, 16), (1, 16))),
        "filter_raw": centred(arg_keys[4], (FILTERS, LEN), 1.0, 6.0, ((0, 16),), jnp.float32),
    }


def reference(query, key_in, value, grad_out, filter_raw):
    total = 2 * LEN
    inv_root = 1.0 / math.sqrt(LEN)
    filt = filter_raw * inv_root
    filt_spec = jnp.fft.rfft(filt, n=total, axis=-1)
    gated = (key_in.astype(jnp.float32) * value.astype(jnp.float32)).astype(jnp.bfloat16)
    dconv = (grad_out.astype(jnp.float32) * query.astype(jnp.float32)).astype(jnp.bfloat16)
    gated_groups = gated.reshape(N_TP, FILTERS, LEN)
    dconv_groups = dconv.reshape(N_TP, FILTERS, LEN)

    def one_group(carry, pieces):
        gated_part, dconv_part = pieces
        gated_spec = jnp.fft.rfft(gated_part.astype(jnp.float32), n=total, axis=-1)
        dconv_spec = jnp.fft.rfft(dconv_part.astype(jnp.float32), n=total, axis=-1)
        conv = jnp.fft.irfft(filt_spec * gated_spec, n=total, axis=-1)[:, :LEN]
        dgated = jnp.fft.irfft(dconv_spec * jnp.conj(filt_spec), n=total, axis=-1)[:, :LEN]
        cross = jnp.fft.irfft(dconv_spec * jnp.conj(gated_spec), n=total, axis=-1)[:, :LEN]
        return (carry + cross * inv_root, (conv.astype(jnp.bfloat16), dgated.astype(jnp.bfloat16)))
    start = jnp.zeros((FILTERS, LEN), jnp.float32)
    filter_grad, outputs = lax.scan(one_group, start, (gated_groups, dconv_groups))
    conv = outputs[0].reshape(C, LEN)
    dgated = outputs[1].reshape(C, LEN)
    grad_query = (grad_out.astype(jnp.float32) * conv.astype(jnp.float32)).astype(jnp.bfloat16)
    grad_key = (dgated.astype(jnp.float32) * value.astype(jnp.float32)).astype(jnp.bfloat16)
    grad_value = (dgated.astype(jnp.float32) * key_in.astype(jnp.float32)).astype(jnp.bfloat16)
    return (grad_query, grad_key, grad_value, filter_grad)
```

```python
import functools
import math

import jax
import jax.numpy as jnp
import ml_dtypes
import numpy as np
from jax import lax
from jax.experimental import pallas as pl
from jax.experimental.pallas import tpu as pltpu
from jax.sharding import PartitionSpec as P

LANES = 128
VMEM_LIMIT = 56 * 2**20
f32 = jnp.float32
bf16 = jnp.bfloat16


def split_parts(table):
    high = table.astype(np.float32).astype(ml_dtypes.bfloat16)
    low = (table - high.astype(np.float64)).astype(np.float32).astype(ml_dtypes.bfloat16)
    return high, low


@functools.lru_cache(maxsize=None)
def make_tables(length):
    rows = length // LANES
    total = 2 * length
    a = np.arange(rows, dtype=np.float64)
    k1 = np.arange(rows, dtype=np.float64) + 0.5
    b = np.arange(LANES, dtype=np.float64)
    first = 2.0 * np.pi * np.outer(k1, a) / (2 * rows)
    turn = 2.0 * np.pi * np.outer(k1, b) / total
    second = 2.0 * np.pi * np.outer(b, b) / LANES
    c2, s2 = np.cos(second), np.sin(second)
    w_high, w_low = split_parts(np.concatenate([np.cos(first), -np.sin(first)], 0))
    m_high, m_low = split_parts(np.block([[c2, -s2], [s2, c2]]))
    mi_high, mi_low = split_parts(np.block([[c2, s2], [-s2, c2]]))
    wi_high, wi_low = split_parts(np.concatenate([np.cos(first).T, -np.sin(first).T], 1))
    scale = 2.0 / total
    return dict(
        w=np.concatenate([w_high, w_low, w_high], 1),
        m=np.concatenate([m_high, m_low, m_high], 0),
        mi=np.concatenate([mi_high, mi_low], 0),
        wi=np.concatenate([wi_high, wi_low], 1),
        turn_cos=np.cos(turn).astype(np.float32),
        turn_sin=np.sin(turn).astype(np.float32),
        back_cos=(scale * np.cos(turn)).astype(np.float32),
        back_sin=(scale * np.sin(turn)).astype(np.float32),
    )


def dot(x, y):
    return jnp.dot(x, y, preferred_element_type=f32)


def whole(table):
    return pl.BlockSpec(table.shape, lambda *_: (0,) * table.ndim)


def params(grid_rank):
    return pltpu.CompilerParams(
        dimension_semantics=("arbitrary",) * grid_rank, vmem_limit_bytes=VMEM_LIMIT
    )


def gate_kernel(q_ref, k_ref, v_ref, g_ref, out_ref, s0, s1):
    group, length = k_ref.shape
    cuts = length // LANES
    for j in range(cuts):
        lanes = slice(j * LANES, (j + 1) * LANES)
        rows = slice(j * group, (j + 1) * group)
        s0[rows, :] = k_ref[:, lanes].astype(f32) * v_ref[:, lanes].astype(f32)
        s1[rows, :] = g_ref[:, lanes].astype(f32) * q_ref[:, lanes].astype(f32)
    for c in range(group):
        out_ref[0, 0, c] = s0[pl.ds(c, cuts, stride=group), :].astype(bf16)
        out_ref[0, 1, c] = s1[pl.ds(c, cuts, stride=group), :].astype(bf16)


def gate(query, key_in, value, grad_out, n):
    channels, length = query.shape
    group = channels // n
    cuts = length // LANES
    spec = pl.BlockSpec((group, length), lambda i: (i, 0))
    return pl.pallas_call(
        gate_kernel,
        grid=(n,),
        in_specs=[spec] * 4,
        out_specs=pl.BlockSpec((1, 2, group, cuts, LANES), lambda i: (i, 0, 0, 0, 0)),
        out_shape=jax.ShapeDtypeStruct((n, 2, group, cuts, LANES), bf16),
        scratch_shapes=[pltpu.VMEM((group * cuts, LANES), f32)] * 2,
        compiler_params=params(1),
        cost_estimate=pl.CostEstimate(
            flops=2 * channels * length, bytes_accessed=12 * channels * length, transcendentals=0
        ),
        name="gate",
    )(query, key_in, value, grad_out)


def finish_kernel(tok_ref, k_ref, v_ref, g_ref, gq_ref, gk_ref, gv_ref, s0, s1):
    group, length = k_ref.shape
    cuts = length // LANES
    for c in range(group):
        rows = slice(c * cuts, (c + 1) * cuts)
        s0[rows, :] = tok_ref[0, 0, c].astype(f32)
        s1[rows, :] = tok_ref[0, 1, c].astype(f32)
    for j in range(cuts):
        lanes = slice(j * LANES, (j + 1) * LANES)
        conv = s0[pl.ds(j, group, stride=cuts), :]
        dgated = s1[pl.ds(j, group, stride=cuts), :]
        gq_ref[:, lanes] = (g_ref[:, lanes].astype(f32) * conv).astype(bf16)
        gk_ref[:, lanes] = (dgated * v_ref[:, lanes].astype(f32)).astype(bf16)
        gv_ref[:, lanes] = (dgated * k_ref[:, lanes].astype(f32)).astype(bf16)


def finish(tok, key_in, value, grad_out):
    n, _, group, cuts, _ = tok.shape
    channels, length = key_in.shape
    spec = pl.BlockSpec((group, length), lambda i: (i, 0))
    return pl.pallas_call(
        finish_kernel,
        grid=(n,),
        in_specs=[pl.BlockSpec((1, 2, group, cuts, LANES), lambda i: (i, 0, 0, 0, 0))] + [spec] * 3,
        out_specs=[spec] * 3,
        out_shape=[jax.ShapeDtypeStruct((channels, length), bf16)] * 3,
        scratch_shapes=[pltpu.VMEM((group * cuts, LANES), f32)] * 2,
        compiler_params=params(1),
        cost_estimate=pl.CostEstimate(
            flops=3 * channels * length, bytes_accessed=16 * channels * length, transcendentals=0
        ),
        name="finish",
    )(tok, key_in, value, grad_out)


def turned(stage, turn_cos, turn_sin, rows, at):
    lanes = slice(at * LANES, (at + 1) * LANES)
    re, im = stage[:rows, lanes], stage[rows:, lanes]
    return jnp.concatenate([re * turn_cos + im * turn_sin, im * turn_cos - re * turn_sin], 1)


def filter_kernel(x_ref, w_ref, m_ref, tc_ref, ts_ref, out_ref, *, scale):
    pair, rows, _ = x_ref.shape
    x = jnp.concatenate([x_ref[i] for i in range(pair)], 1)
    high = x.astype(bf16)
    low = (x - high.astype(f32)).astype(bf16)
    stage = dot(w_ref[...], jnp.concatenate([high, high, low], 0))
    for i in range(pair):
        u = turned(stage, tc_ref[...], ts_ref[...], rows, i) * scale
        u_high = u.astype(bf16)
        u_low = (u - u_high.astype(f32)).astype(bf16)
        out_ref[i] = dot(jnp.concatenate([u_high, u_high, u_low], 1), m_ref[...])


def filter_spectrum(filt, t, scale):
    n, rows, _ = filt.shape
    pair = 2
    tables = [t["w"], t["m"], t["turn_cos"], t["turn_sin"]]
    return pl.pallas_call(
        functools.partial(filter_kernel, scale=scale),
        grid=(n // pair,),
        in_specs=[pl.BlockSpec((pair, rows, LANES), lambda i: (i, 0, 0))] + [whole(x) for x in tables],
        out_specs=pl.BlockSpec((pair, rows, 2 * LANES), lambda i: (i, 0, 0)),
        out_shape=jax.ShapeDtypeStruct((n, rows, 2 * LANES), f32),
        compiler_params=params(1),
        cost_estimate=pl.CostEstimate(
            flops=12 * n * rows * LANES * 512, bytes_accessed=16 * n * rows * LANES, transcendentals=0
        ),
        name="filter_spectrum",
    )(filt, *tables)


def back(spec, mi_ref, wi_ref, bc, bs, pair, rows):
    stage = dot(jnp.concatenate([spec, spec], 1), mi_ref[...])
    re_parts, im_parts = [], []
    for i in range(pair):
        re = stage[i * rows : (i + 1) * rows, :LANES]
        im = stage[i * rows : (i + 1) * rows, LANES:]
        re_parts.append((re * bc - im * bs).astype(bf16))
        im_parts.append((re * bs + im * bc).astype(bf16))
    v = jnp.concatenate([jnp.concatenate(re_parts, 1), jnp.concatenate(im_parts, 1)], 0)
    return dot(wi_ref[...], jnp.concatenate([v, v], 0))


def spectra_kernel(
    x_ref, f_ref, w_ref, m_ref, tc_ref, ts_ref, mi_ref, wi_ref, bc_ref, bs_ref,
    cross_ref, conv_ref, dgated_ref, *, scale,
):
    n, _, pair, cuts, _ = x_ref.shape
    rows = n * cuts
    x = jnp.concatenate(
        [x_ref[:, s, i].reshape(rows, LANES) for s in range(2) for i in range(pair)], 1
    )
    stage = dot(w_ref[:, : 2 * rows], jnp.concatenate([x, x], 0))
    u = jnp.concatenate(
        [turned(stage, tc_ref[...], ts_ref[...], rows, i).astype(bf16) for i in range(2 * pair)], 0
    )
    spec = dot(jnp.concatenate([u, u], 1), m_ref[: 4 * LANES, :])
    half = pair * rows
    gr, gi = spec[:half, :LANES], spec[:half, LANES:]
    dr, di = spec[half:, :LANES], spec[half:, LANES:]
    cross = jnp.concatenate([dr * gr + di * gi, di * gr - dr * gi], 1).astype(bf16)
    f = f_ref[...].reshape(half, 2 * LANES)
    fr, fi = f[:, :LANES], f[:, LANES:]
    conv_ref[...] = (
        jnp.concatenate([fr * gr - fi * gi, fr * gi + fi * gr], 1).astype(bf16).reshape(conv_ref.shape)
    )
    dgated_ref[...] = (
        jnp.concatenate([dr * fr + di * fi, di * fr - dr * fi], 1).astype(bf16).reshape(dgated_ref.shape)
    )
    out = back(cross, mi_ref, wi_ref, bc_ref[...] * scale, bs_ref[...] * scale, pair, rows)
    runs, halves = cross_ref.shape[:2]
    for h in range(halves):
        for z in range(runs):
            at = (h * runs + z) * cuts
            for i in range(pair):
                cross_ref[z, h, i] = out[at : at + cuts, i * LANES : (i + 1) * LANES]


def spectra(x, f, t, scale, runs, halves):
    n, _, group, cuts, _ = x.shape
    rows = n * cuts
    pair = 2
    tables = [t[k] for k in ("w", "m", "turn_cos", "turn_sin", "mi", "wi", "back_cos", "back_sin")]
    spec_block = pl.BlockSpec((pair, rows, 2 * LANES), lambda i: (i, 0, 0))
    return pl.pallas_call(
        functools.partial(spectra_kernel, scale=scale),
        grid=(group // pair,),
        in_specs=[pl.BlockSpec((n, 2, pair, cuts, LANES), lambda i: (0, 0, i, 0, 0)), spec_block]
        + [whole(v) for v in tables],
        out_specs=[
            pl.BlockSpec((runs, halves, pair, cuts, LANES), lambda i: (0, 0, i, 0, 0)),
            spec_block,
            spec_block,
        ],
        out_shape=[
            jax.ShapeDtypeStruct((runs, halves, group, cuts, LANES), f32),
            jax.ShapeDtypeStruct((group, rows, 2 * LANES), bf16),
            jax.ShapeDtypeStruct((group, rows, 2 * LANES), bf16),
        ],
        compiler_params=params(1),
        cost_estimate=pl.CostEstimate(
            flops=24 * group * rows * LANES * 512, bytes_accessed=32 * group * rows * LANES, transcendentals=0
        ),
        name="spectra",
    )(x, f, *tables)


def signals_kernel(conv_ref, dgated_ref, mi_ref, wi_ref, bc_ref, bs_ref, out_ref):
    n, _, pair, cuts, _ = out_ref.shape
    rows = n * cuts
    both = jnp.concatenate(
        [r[...].reshape(pair * rows, 2 * LANES) for r in (conv_ref, dgated_ref)], 0
    )
    out = back(both, mi_ref, wi_ref, bc_ref[...], bs_ref[...], 2 * pair, rows).astype(bf16)
    for s in range(2):
        for i in range(pair):
            lanes = slice((s * pair + i) * LANES, (s * pair + i + 1) * LANES)
            out_ref[:, s, i] = out[:, lanes].reshape(n, cuts, LANES)


def signals(conv, dgated, t, n):
    group, rows, _ = conv.shape
    cuts = rows // n
    pair = 2
    tables = [t[k] for k in ("mi", "wi", "back_cos", "back_sin")]
    spec_block = pl.BlockSpec((pair, rows, 2 * LANES), lambda i: (i, 0, 0))
    return pl.pallas_call(
        signals_kernel,
        grid=(group // pair,),
        in_specs=[spec_block] * 2 + [whole(v) for v in tables],
        out_specs=pl.BlockSpec((n, 2, pair, cuts, LANES), lambda i: (0, 0, i, 0, 0)),
        out_shape=jax.ShapeDtypeStruct((n, 2, group, cuts, LANES), bf16),
        compiler_params=params(1),
        cost_estimate=pl.CostEstimate(
            flops=16 * group * rows * LANES * 512, bytes_accessed=12 * group * rows * LANES, transcendentals=0
        ),
        name="signals",
    )(conv, dgated, *tables)


def body(query, key_in, value, grad_out, filter_raw, *, n_ctx, n_tp):
    group, length = filter_raw.shape
    rows = length // LANES
    root = 1.0 / math.sqrt(length)
    t = {k: jnp.asarray(v) for k, v in make_tables(length).items()}
    halves = 2
    runs = n_tp // halves

    sent = gate(query, key_in, value, grad_out, n_ctx)
    got = lax.all_to_all(sent, "ctx", split_axis=0, concat_axis=0, tiled=True)
    filt = filter_spectrum(filter_raw.reshape(group, rows, LANES), t, root)
    cross, conv, dgated = spectra(got, filt, t, root, runs, halves)
    near = [[h * runs + z for z in range(runs)] for h in range(halves)]
    part = lax.psum_scatter(cross, "tp", scatter_dimension=0, tiled=True, axis_index_groups=near)
    tok = lax.all_to_all(signals(conv, dgated, t, n_ctx), "ctx", split_axis=0, concat_axis=0, tiled=True)
    grad_query, grad_key, grad_value = finish(tok, key_in, value, grad_out)
    side = lax.axis_index("tp") // runs
    mine = lax.dynamic_index_in_dim(part[0], side, 0, keepdims=False)
    other = lax.dynamic_index_in_dim(part[0], 1 - side, 0, keepdims=False)
    far = [(i, (i + runs) % n_tp) for i in range(n_tp)]
    filter_grad = (mine + lax.ppermute(other, "tp", far)).reshape(group, length // n_tp)
    return (grad_query, grad_key, grad_value, filter_grad)


def solution(mesh):
    placed = (P("tp", "ctx"), P("tp", "ctx"), P("tp", "ctx"), P("tp", "ctx"), P("ctx", None))
    return jax.shard_map(
        functools.partial(body, n_ctx=mesh.shape["ctx"], n_tp=mesh.shape["tp"]),
        mesh=mesh,
        in_specs=placed,
        out_specs=(P("tp", "ctx"), P("tp", "ctx"), P("tp", "ctx"), P("ctx", "tp")),
        check_vma=False,
    )
```

```python
import functools
import math

import jax
import jax.numpy as jnp
import ml_dtypes
import numpy as np
from jax import lax
from jax.experimental import pallas as pl
from jax.experimental.pallas import tpu as pltpu
from jax.sharding import PartitionSpec as P

LANES = 128
VMEM_LIMIT = 56 * 2**20
TOKEN_STEPS = 4
PAIR = 8
CROSS_BACK = ("mi2", "wi2")
TOKEN_BACK = ("mi", "wi")
f32 = jnp.float32
bf16 = jnp.bfloat16


def split_parts(table):
    high = table.astype(np.float32).astype(ml_dtypes.bfloat16)
    low = (table - high.astype(np.float64)).astype(np.float32).astype(ml_dtypes.bfloat16)
    return high, low


@functools.lru_cache(maxsize=None)
def make_tables(length):
    rows = length // LANES
    total = 2 * length
    a = np.arange(rows, dtype=np.float64)
    k1 = np.arange(rows, dtype=np.float64) + 0.5
    b = np.arange(LANES, dtype=np.float64)
    first = 2.0 * np.pi * np.outer(k1, a) / (2 * rows)
    turn = 2.0 * np.pi * np.outer(k1, b) / total
    second = 2.0 * np.pi * np.outer(b, b) / LANES
    c2, s2 = np.cos(second), np.sin(second)
    w_high, w_low = split_parts(np.concatenate([np.cos(first), -np.sin(first)], 0))
    m_high, m_low = split_parts(np.block([[c2, -s2], [s2, c2]]))
    mi_high, mi_low = split_parts(np.block([[c2, s2], [-s2, c2]]))
    wi_high, wi_low = split_parts(np.concatenate([np.cos(first).T, -np.sin(first).T], 1))
    return dict(
        w3=np.concatenate([w_high, w_low, w_high], 1),
        m3=np.concatenate([m_high, m_low, m_high], 0),
        w=w_high,
        m=m_high,
        mi=mi_high,
        wi=wi_high,
        mi2=np.concatenate([mi_high, mi_low], 0),
        wi2=np.concatenate([wi_high, wi_low], 1),
        turn_cos=np.cos(turn).astype(np.float32),
        turn_sin=np.sin(turn).astype(np.float32),
    )


def dot(x, y):
    return jnp.dot(x, y, preferred_element_type=f32)


def whole(table):
    return pl.BlockSpec(table.shape, lambda *_: (0,) * table.ndim)


def params(grid_rank, limit=VMEM_LIMIT):
    return pltpu.CompilerParams(
        dimension_semantics=("arbitrary",) * grid_rank if grid_rank else None,
        vmem_limit_bytes=limit,
    )


def swap_table(size):
    index = np.arange(size * size).reshape(size, size)
    table = np.zeros((size * size, size * size), np.float32)
    table[index.T.reshape(-1), index.reshape(-1)] = 1.0
    return table.astype(ml_dtypes.bfloat16)


def copies(pairs, sems, at):
    return [pltpu.make_async_copy(src, dst, sems.at[at, i]) for i, (src, dst) in enumerate(pairs)]


def start(moves):
    for move in moves:
        move.start()


def wait(moves):
    for move in moves:
        move.wait()


ANY = pl.BlockSpec(memory_space=pl.ANY)
VMEM = pl.BlockSpec(memory_space=pltpu.VMEM)


def gate_kernel(q_ref, k_ref, v_ref, g_ref, swap_ref, out_ref, q, k, v, g, o, in_sems, out_sems):
    n, _, group, cuts, _ = out_ref.shape
    runs = n // TOKEN_STEPS

    def loads(step):
        rows = pl.ds(step * runs * group, runs * group)
        pairs = [(r.at[rows], s.at[rows]) for r, s in ((k_ref, k), (v_ref, v), (g_ref, g), (q_ref, q))]
        return copies(pairs, in_sems, step)

    def stores(step):
        at = pl.ds(step * runs, runs)
        return copies([(o.at[at], out_ref.at[at])], out_sems, step)

    for step in range(TOKEN_STEPS):
        start(loads(step))
    for step in range(TOKEN_STEPS):
        wait(loads(step))
        for run in range(step * runs, (step + 1) * runs):
            rows = slice(run * group, (run + 1) * group)

            def product(x, y):
                z = (x[rows, :].astype(f32) * y[rows, :].astype(f32)).astype(bf16)
                return jnp.concatenate([z[:, j * LANES : (j + 1) * LANES] for j in range(cuts)], 0)

            both = jnp.concatenate([product(k, v), product(g, q)], 1)
            out = dot(swap_ref[...], both).astype(bf16)
            for s in range(2):
                o[run, s] = out[:, s * LANES : (s + 1) * LANES].reshape(group, cuts, LANES)
        start(stores(step))
    for step in range(TOKEN_STEPS):
        wait(stores(step))


def gate(query, key_in, value, grad_out, n):
    channels, length = query.shape
    group = channels // n
    cuts = length // LANES
    swap = jnp.asarray(swap_table(group))
    sent = (n, 2, group, cuts, LANES)
    return pl.pallas_call(
        gate_kernel,
        in_specs=[ANY] * 4 + [VMEM],
        out_specs=ANY,
        out_shape=jax.ShapeDtypeStruct(sent, bf16),
        scratch_shapes=[pltpu.VMEM(query.shape, bf16)] * 4
        + [pltpu.VMEM(sent, bf16), pltpu.SemaphoreType.DMA((TOKEN_STEPS, 4)), pltpu.SemaphoreType.DMA((TOKEN_STEPS, 1))],
        compiler_params=params(0),
        cost_estimate=pl.CostEstimate(
            flops=2 * channels * length, bytes_accessed=12 * channels * length, transcendentals=0
        ),
        name="gate",
    )(query, key_in, value, grad_out, swap)


def finish_kernel(
    tok_ref, k_ref, v_ref, g_ref, swap_ref, gq_ref, gk_ref, gv_ref, tok, k, v, g, gq, gk, gv, in_sems, out_sems
):
    n, _, group, cuts, _ = tok_ref.shape
    runs = n // TOKEN_STEPS

    def loads(step):
        rows = pl.ds(step * runs * group, runs * group)
        at = pl.ds(step * runs, runs)
        pairs = [(tok_ref.at[at], tok.at[at])]
        pairs += [(r.at[rows], s.at[rows]) for r, s in ((g_ref, g), (v_ref, v), (k_ref, k))]
        return copies(pairs, in_sems, step)

    def stores(step):
        rows = pl.ds(step * runs * group, runs * group)
        pairs = [(s.at[rows], r.at[rows]) for r, s in ((gq_ref, gq), (gk_ref, gk), (gv_ref, gv))]
        return copies(pairs, out_sems, step)

    for step in range(TOKEN_STEPS):
        start(loads(step))
    for step in range(TOKEN_STEPS):
        wait(loads(step))
        for run in range(step * runs, (step + 1) * runs):
            rows = slice(run * group, (run + 1) * group)
            both = jnp.concatenate([tok[run, s].reshape(group * cuts, LANES) for s in range(2)], 1)
            out = dot(swap_ref[...], both)
            for j in range(cuts):
                lanes = slice(j * LANES, (j + 1) * LANES)
                conv = out[j * group : (j + 1) * group, :LANES]
                dgated = out[j * group : (j + 1) * group, LANES:]
                gq[rows, lanes] = (g[rows, lanes].astype(f32) * conv).astype(bf16)
                gk[rows, lanes] = (dgated * v[rows, lanes].astype(f32)).astype(bf16)
                gv[rows, lanes] = (dgated * k[rows, lanes].astype(f32)).astype(bf16)
        start(stores(step))
    for step in range(TOKEN_STEPS):
        wait(stores(step))


def finish(tok, key_in, value, grad_out):
    group = tok.shape[2]
    channels, length = key_in.shape
    swap = jnp.asarray(swap_table(group))
    return pl.pallas_call(
        finish_kernel,
        in_specs=[ANY] * 4 + [VMEM],
        out_specs=[ANY] * 3,
        out_shape=[jax.ShapeDtypeStruct((channels, length), bf16)] * 3,
        scratch_shapes=[pltpu.VMEM(tok.shape, bf16)]
        + [pltpu.VMEM(key_in.shape, bf16)] * 6
        + [pltpu.SemaphoreType.DMA((TOKEN_STEPS, 4)), pltpu.SemaphoreType.DMA((TOKEN_STEPS, 3))],
        compiler_params=params(0, 50 * 2**20),
        cost_estimate=pl.CostEstimate(
            flops=3 * channels * length, bytes_accessed=16 * channels * length, transcendentals=0
        ),
        name="finish",
    )(tok, key_in, value, grad_out, swap)


def turned(stage, turn_cos, turn_sin, rows, at):
    lanes = slice(at * LANES, (at + 1) * LANES)
    re, im = stage[:rows, lanes], stage[rows:, lanes]
    return jnp.concatenate([re * turn_cos + im * turn_sin, im * turn_cos - re * turn_sin], 1)


def filter_kernel(x_ref, w_ref, m_ref, tc_ref, ts_ref, out_ref, *, scale):
    pair, rows, _ = x_ref.shape
    x = jnp.concatenate([x_ref[i] for i in range(pair)], 1)
    high = x.astype(bf16)
    low = (x - high.astype(f32)).astype(bf16)
    stage = dot(w_ref[...], jnp.concatenate([high, high, low], 0))
    for i in range(pair):
        u = turned(stage, tc_ref[...], ts_ref[...], rows, i) * scale
        u_high = u.astype(bf16)
        u_low = (u - u_high.astype(f32)).astype(bf16)
        out_ref[i] = dot(jnp.concatenate([u_high, u_high, u_low], 1), m_ref[...])


def filter_spectrum(filt, t, scale):
    n, rows, _ = filt.shape
    pair = 2
    tables = [t["w3"], t["m3"], t["turn_cos"], t["turn_sin"]]
    return pl.pallas_call(
        functools.partial(filter_kernel, scale=scale),
        grid=(n // pair,),
        in_specs=[pl.BlockSpec((pair, rows, LANES), lambda i: (i, 0, 0))] + [whole(x) for x in tables],
        out_specs=pl.BlockSpec((pair, rows, 2 * LANES), lambda i: (i, 0, 0)),
        out_shape=jax.ShapeDtypeStruct((n, rows, 2 * LANES), f32),
        compiler_params=params(1),
        cost_estimate=pl.CostEstimate(
            flops=12 * n * rows * LANES * 512, bytes_accessed=16 * n * rows * LANES, transcendentals=0
        ),
        name="filter_spectrum",
    )(filt, *tables)


def back(spec, mi_ref, wi_ref, bc, bs, pair, rows):
    parts = mi_ref.shape[0] // (2 * LANES)
    stage = dot(jnp.concatenate([spec] * parts, 1), mi_ref[...])
    re_parts, im_parts = [], []
    for i in range(pair):
        re = stage[i * rows : (i + 1) * rows, :LANES]
        im = stage[i * rows : (i + 1) * rows, LANES:]
        re_parts.append((re * bc - im * bs).astype(bf16))
        im_parts.append((re * bs + im * bc).astype(bf16))
    v = jnp.concatenate([jnp.concatenate(re_parts, 1), jnp.concatenate(im_parts, 1)], 0)
    return dot(wi_ref[...], jnp.concatenate([v] * parts, 0))


def spectra_kernel(
    place_ref, x_ref, f_ref, w_hbm, m_hbm, tc_hbm, ts_hbm, mi_hbm, wi_hbm,
    stay_ref, leave0_ref, leave1_ref, conv_ref, dgated_ref,
    x_buf, f_buf, cross_buf, conv_buf, dgated_buf, w_ref, m_ref, tc_ref, ts_ref, mi_ref, wi_ref,
    in_sems, out_sems, leave_sems, table_sems, *, scale,
):
    n, _, group, cuts, _ = x_ref.shape
    pair = x_buf.shape[3]
    rows = n * cuts
    steps = group // pair
    _, _, ring, halves = cross_buf.shape[:4]

    def loads(step):
        at = pl.ds(step * pair, pair)
        return copies([(x_ref.at[:, :, at], x_buf.at[step]), (f_ref.at[at], f_buf.at[step])], in_sems, step)

    def stores(step):
        at = pl.ds(step * pair, pair)
        pairs = [(cross_buf.at[step, 0], stay_ref.at[step])]
        pairs += [(conv_buf.at[step], conv_ref.at[at]), (dgated_buf.at[step], dgated_ref.at[at])]
        return copies(pairs, out_sems, step)

    def leaving(step, leave_ref):
        return copies([(cross_buf.at[step, 1], leave_ref)], leave_sems, step)

    tables = copies(
        [(w_hbm, w_ref), (tc_hbm, tc_ref), (ts_hbm, ts_ref), (m_hbm, m_ref), (mi_hbm, mi_ref), (wi_hbm, wi_ref)],
        table_sems, 0,
    )
    start(loads(0))
    start(tables)
    for step in range(1, steps):
        start(loads(step))
    wait(tables)

    @pl.loop(0, steps)
    def _(step):
        wait(loads(step))
        x = jnp.concatenate(
            [x_buf[step, :, s, i].reshape(rows, LANES) for s in range(2) for i in range(pair)], 1
        )
        stage = dot(w_ref[...], x)
        u = jnp.concatenate(
            [turned(stage, tc_ref[...], ts_ref[...], rows, i).astype(bf16) for i in range(2 * pair)], 0
        )
        spec = dot(u, m_ref[...])
        half = pair * rows
        gr, gi = spec[:half, :LANES], spec[:half, LANES:]
        dr, di = spec[half:, :LANES], spec[half:, LANES:]
        cross = (jnp.concatenate([dr * gr + di * gi, di * gr - dr * gi], 1) * scale).astype(bf16)
        f = f_buf[step].reshape(half, 2 * LANES)
        fr, fi = f[:, :LANES], f[:, LANES:]
        conv_buf[step] = (
            jnp.concatenate([fr * gr - fi * gi, fr * gi + fi * gr], 1).astype(bf16).reshape(pair, rows, 2 * LANES)
        )
        dgated_buf[step] = (
            jnp.concatenate([dr * fr + di * fi, di * fr - dr * fi], 1).astype(bf16).reshape(pair, rows, 2 * LANES)
        )
        out = back(cross, mi_ref, wi_ref, tc_ref[...], ts_ref[...], pair, rows)
        for place in range(2 * ring * halves):
            at = place * cuts
            side, turns, half = order(place, 2 * ring * halves, step)
            to = (side ^ place_ref[step, 0], (turns - place_ref[step, 1]) & (ring - 1), half ^ place_ref[step, 2])
            for i in range(pair):
                cross_buf[step, *to, i] = out[at : at + cuts, i * LANES : (i + 1) * LANES].astype(bf16)
        start(stores(step))
        for one, leave_ref in enumerate((leave0_ref, leave1_ref)):

            @pl.when(step == one)
            def _():
                start(leaving(one, leave_ref))

    for step in range(steps):
        wait(stores(step))
    for one, leave_ref in enumerate((leave0_ref, leave1_ref)):
        wait(leaving(one, leave_ref))


def spectra(place, x, f, t, scale, n_tp):
    n, _, group, cuts, _ = x.shape
    rows = n * cuts
    pair = PAIR
    steps = group // pair
    tables = [t[k] for k in ("w", "m", "turn_cos", "turn_sin", CROSS_BACK[0], CROSS_BACK[1])]
    spec = (pair, rows, 2 * LANES)
    kept = (n_tp // 4, 2, pair, cuts, LANES)
    return pl.pallas_call(
        functools.partial(spectra_kernel, scale=scale),
        in_specs=[pl.BlockSpec(memory_space=pltpu.SMEM)] + [ANY] * (2 + len(tables)),
        out_specs=[ANY] * 5,
        out_shape=[
            jax.ShapeDtypeStruct((steps, *kept), bf16),
            jax.ShapeDtypeStruct(kept, bf16),
            jax.ShapeDtypeStruct(kept, bf16),
            jax.ShapeDtypeStruct((group, rows, 2 * LANES), bf16),
            jax.ShapeDtypeStruct((group, rows, 2 * LANES), bf16),
        ],
        scratch_shapes=[
            pltpu.VMEM((steps, n, 2, pair, cuts, LANES), bf16),
            pltpu.VMEM((steps, *spec), f32),
            pltpu.VMEM((steps, 2, *kept), bf16),
            pltpu.VMEM((steps, *spec), bf16),
            pltpu.VMEM((steps, *spec), bf16),
            *[pltpu.VMEM(v.shape, v.dtype) for v in tables],
            pltpu.SemaphoreType.DMA((steps, 2)),
            pltpu.SemaphoreType.DMA((steps, 3)),
            pltpu.SemaphoreType.DMA((steps, 1)),
            pltpu.SemaphoreType.DMA((1, len(tables))),
        ],
        compiler_params=params(0),
        cost_estimate=pl.CostEstimate(
            flops=24 * group * rows * LANES * 512, bytes_accessed=32 * group * rows * LANES, transcendentals=0
        ),
        name="spectra",
    )(place, x, f, *tables)


def signals_kernel(
    conv_ref, dgated_ref, mi_hbm, wi_hbm, tc_hbm, ts_hbm, out_ref,
    spec_buf, out_buf, mi_ref, wi_ref, tc_ref, ts_ref, in_sems, out_sems, table_sems,
):
    n, _, group, cuts, _ = out_ref.shape
    steps, _, pair, rows, _ = spec_buf.shape

    def loads(step):
        at = pl.ds(step * pair, pair)
        pairs = [(conv_ref.at[at], spec_buf.at[step, 0]), (dgated_ref.at[at], spec_buf.at[step, 1])]
        return copies(pairs, in_sems, step)

    def stores(step):
        return copies([(out_buf.at[step], out_ref.at[:, :, pl.ds(step * pair, pair)])], out_sems, step)

    tables = copies(
        [(mi_hbm, mi_ref), (tc_hbm, tc_ref), (ts_hbm, ts_ref), (wi_hbm, wi_ref)], table_sems, 0
    )
    start(loads(0))
    start(tables)
    for step in range(1, steps):
        start(loads(step))
    wait(tables)

    @pl.loop(0, steps)
    def _(step):
        wait(loads(step))
        both = spec_buf[step].reshape(2 * pair * rows, 2 * LANES)
        out = back(both, mi_ref, wi_ref, tc_ref[...], ts_ref[...], 2 * pair, rows).astype(bf16)
        for s in range(2):
            for i in range(pair):
                lanes = slice((s * pair + i) * LANES, (s * pair + i + 1) * LANES)
                out_buf[step, :, s, i] = out[:, lanes].reshape(n, cuts, LANES)
        start(stores(step))

    for step in range(steps):
        wait(stores(step))


def signals(conv, dgated, t, n):
    group, rows, _ = conv.shape
    cuts = rows // n
    pair = PAIR
    steps = group // pair
    tables = [t[k] for k in (*TOKEN_BACK, "turn_cos", "turn_sin")]
    return pl.pallas_call(
        signals_kernel,
        in_specs=[ANY] * (2 + len(tables)),
        out_specs=ANY,
        out_shape=jax.ShapeDtypeStruct((n, 2, group, cuts, LANES), bf16),
        scratch_shapes=[
            pltpu.VMEM((steps, 2, pair, rows, 2 * LANES), bf16),
            pltpu.VMEM((steps, n, 2, pair, cuts, LANES), bf16),
            *[pltpu.VMEM(v.shape, v.dtype) for v in tables],
            pltpu.SemaphoreType.DMA((steps, 2)),
            pltpu.SemaphoreType.DMA((steps, 1)),
            pltpu.SemaphoreType.DMA((1, len(tables))),
        ],
        compiler_params=params(0),
        cost_estimate=pl.CostEstimate(
            flops=16 * group * rows * LANES * 512, bytes_accessed=12 * group * rows * LANES, transcendentals=0
        ),
        name="signals",
    )(conv, dgated, *tables)


def order(place, n, shift):
    runs = n // 2
    half, z = place // runs, (place + shift) % runs
    return z % 2, z // 2, half


def sum_ring(stay, got, n):
    runs = n // 2
    steps = runs // 2
    total = stay[:, 0].astype(f32) + got[:, 0].astype(f32)
    for step in range(1, steps):
        share = (stay[:, step].astype(f32) + got[:, step].astype(f32)).astype(bf16)
        pairs = [(i, i // runs * runs + (i + 2 * step) % runs) for i in range(n)]
        total = total + lax.ppermute(share, "tp", pairs).astype(f32)
    return total


def body(query, key_in, value, grad_out, filter_raw, *, n_ctx, n_tp):
    group, length = filter_raw.shape
    rows = length // LANES
    root = 1.0 / math.sqrt(length)
    runs = n_tp // 2
    t = {k: jnp.asarray(v) for k, v in make_tables(length).items()}

    sent = gate(query, key_in, value, grad_out, n_ctx)
    got = lax.all_to_all(sent, "ctx", split_axis=0, concat_axis=0, tiled=True)
    filt = filter_spectrum(filter_raw.reshape(group, rows, LANES), t, root / length)
    me = lax.axis_index("tp")
    place = jnp.stack([jnp.stack(order(me, n_tp, shift)) for shift in range(2)]).astype(jnp.int32)
    stay, *leave, conv, dgated = spectra(place, got, filt, t, root / length, n_tp)
    near = []
    for shift, x in enumerate(leave):
        pairs = [(i, i // runs * runs + (((i + shift) % runs ^ 1) - shift) % runs) for i in range(n_tp)]
        near.append(lax.ppermute(x, "tp", pairs))
    made = signals(conv, dgated, t, n_ctx)
    made, *near = lax.optimization_barrier((made, *near))
    tok = lax.all_to_all(made, "ctx", split_axis=0, concat_axis=0, tiled=True)
    part = sum_ring(stay, jnp.stack(near), n_tp)
    far = lax.ppermute(part[:, 1], "tp", [(i, (i + runs) % n_tp) for i in range(n_tp)])
    grad_query, grad_key, grad_value = finish(tok, key_in, value, grad_out)
    mine = part[:, 0]
    mine, grad_query = lax.optimization_barrier((mine, grad_query))
    filter_grad = (mine + far).reshape(group, length // n_tp)
    return (grad_query, grad_key, grad_value, filter_grad)


def solution(mesh):
    placed = (P("tp", "ctx"), P("tp", "ctx"), P("tp", "ctx"), P("tp", "ctx"), P("ctx", None))
    return jax.shard_map(
        functools.partial(body, n_ctx=mesh.shape["ctx"], n_tp=mesh.shape["tp"]),
        mesh=mesh,
        in_specs=placed,
        out_specs=(P("tp", "ctx"), P("tp", "ctx"), P("tp", "ctx"), P("ctx", "tp")),
        check_vma=False,
    )
```

```python
import functools
import math

import jax
import jax.numpy as jnp
import ml_dtypes
import numpy as np
from jax import lax
from jax.experimental import pallas as pl
from jax.experimental.pallas import tpu as pltpu
from jax.sharding import PartitionSpec as P

LANES = 128
VMEM_LIMIT = 56 * 2**20
SPLIT = 2
TOKEN_STEPS = 4
FILTERS = 4
FILTER_PAIR = 4
CROSS_BACK = ("mi2", "wi2")
TOKEN_BACK = ("mi", "wi")
f32 = jnp.float32
bf16 = jnp.bfloat16


def split_parts(table):
    high = table.astype(np.float32).astype(ml_dtypes.bfloat16)
    low = (table - high.astype(np.float64)).astype(np.float32).astype(ml_dtypes.bfloat16)
    return high, low


@functools.lru_cache(maxsize=None)
def make_tables(length):
    rows = length // LANES
    total = 2 * length
    a = np.arange(rows, dtype=np.float64)
    k1 = np.arange(rows, dtype=np.float64) + 0.5
    b = np.arange(LANES, dtype=np.float64)
    first = 2.0 * np.pi * np.outer(k1, a) / (2 * rows)
    turn = 2.0 * np.pi * np.outer(k1, b) / total
    second = 2.0 * np.pi * np.outer(b, b) / LANES
    c2, s2 = np.cos(second), np.sin(second)
    w_high, w_low = split_parts(np.concatenate([np.cos(first), -np.sin(first)], 0))
    m_high, m_low = split_parts(np.block([[c2, -s2], [s2, c2]]))
    mi_high, mi_low = split_parts(np.block([[c2, s2], [-s2, c2]]))
    wi_high, wi_low = split_parts(np.concatenate([np.cos(first).T, -np.sin(first).T], 1))
    return dict(
        w3=np.concatenate([w_high, w_low, w_high], 1),
        m3=np.concatenate([m_high, m_low, m_high], 0),
        w=w_high,
        m=m_high,
        mi=mi_high,
        wi=wi_high,
        mi2=np.concatenate([mi_high, mi_low], 0),
        wi2=np.concatenate([wi_high, wi_low], 1),
        turn_cos=np.cos(turn).astype(np.float32),
        turn_sin=np.sin(turn).astype(np.float32),
    )


def dot(x, y):
    return jnp.dot(x, y, preferred_element_type=f32)


def whole(table):
    return pl.BlockSpec(table.shape, lambda *_: (0,) * table.ndim)


def params(grid_rank, limit=VMEM_LIMIT):
    return pltpu.CompilerParams(
        dimension_semantics=("arbitrary",) * grid_rank if grid_rank else None,
        vmem_limit_bytes=limit,
    )


def swap_table(size):
    index = np.arange(size * size).reshape(size, size)
    table = np.zeros((size * size, size * size), np.float32)
    table[index.T.reshape(-1), index.reshape(-1)] = 1.0
    return table.astype(ml_dtypes.bfloat16)


def copies(pairs, sems, at):
    return [pltpu.make_async_copy(src, dst, sems.at[at, i]) for i, (src, dst) in enumerate(pairs)]


def start(moves):
    for move in moves:
        move.start()


def wait(moves):
    for move in moves:
        move.wait()


ANY = pl.BlockSpec(memory_space=pl.ANY)
VMEM = pl.BlockSpec(memory_space=pltpu.VMEM)


def gate_kernel(q_ref, k_ref, v_ref, g_ref, swap_ref, out_ref, q, k, v, g, o, in_sems, out_sems):
    n, split, _, kept, cuts, _ = out_ref.shape
    group = split * kept
    runs = n // TOKEN_STEPS

    def loads(step):
        rows = pl.ds(step * runs * group, runs * group)
        pairs = [(r.at[rows], s.at[rows]) for r, s in ((k_ref, k), (v_ref, v), (g_ref, g), (q_ref, q))]
        return copies(pairs, in_sems, step)

    def stores(step):
        at = pl.ds(step * runs, runs)
        return copies([(o.at[at], out_ref.at[at])], out_sems, step)

    for step in range(TOKEN_STEPS):
        start(loads(step))
    for step in range(TOKEN_STEPS):
        wait(loads(step))
        for run in range(step * runs, (step + 1) * runs):
            rows = slice(run * group, (run + 1) * group)

            def product(x, y):
                z = (x[rows, :].astype(f32) * y[rows, :].astype(f32)).astype(bf16)
                return jnp.concatenate([z[:, j * LANES : (j + 1) * LANES] for j in range(cuts)], 0)

            both = jnp.concatenate([product(k, v), product(g, q)], 1)
            out = dot(swap_ref[...], both).astype(bf16)
            for s in range(2):
                o[run, :, s] = out[:, s * LANES : (s + 1) * LANES].reshape(split, kept, cuts, LANES)
        start(stores(step))
    for step in range(TOKEN_STEPS):
        wait(stores(step))


def gate(query, key_in, value, grad_out, n):
    channels, length = query.shape
    group = channels // n
    cuts = length // LANES
    swap = jnp.asarray(swap_table(group))
    sent = (n, SPLIT, 2, group // SPLIT, cuts, LANES)
    return pl.pallas_call(
        gate_kernel,
        in_specs=[ANY] * 4 + [VMEM],
        out_specs=ANY,
        out_shape=jax.ShapeDtypeStruct(sent, bf16),
        scratch_shapes=[pltpu.VMEM(query.shape, bf16)] * 4
        + [pltpu.VMEM(sent, bf16), pltpu.SemaphoreType.DMA((TOKEN_STEPS, 4)), pltpu.SemaphoreType.DMA((TOKEN_STEPS, 1))],
        compiler_params=params(0),
        cost_estimate=pl.CostEstimate(
            flops=2 * channels * length, bytes_accessed=12 * channels * length, transcendentals=0
        ),
        name="gate",
    )(query, key_in, value, grad_out, swap)


def finish_kernel(
    tok_ref, k_ref, v_ref, g_ref, swap_ref, gq_ref, gk_ref, gv_ref, tok, k, v, g, gq, gk, gv, in_sems, out_sems
):
    n, split, _, kept, cuts, _ = tok_ref.shape
    group = split * kept
    runs = n // TOKEN_STEPS

    def loads(step):
        rows = pl.ds(step * runs * group, runs * group)
        at = pl.ds(step * runs, runs)
        pairs = [(tok_ref.at[at], tok.at[at])]
        pairs += [(r.at[rows], s.at[rows]) for r, s in ((g_ref, g), (v_ref, v), (k_ref, k))]
        return copies(pairs, in_sems, step)

    def stores(step):
        rows = pl.ds(step * runs * group, runs * group)
        pairs = [(s.at[rows], r.at[rows]) for r, s in ((gq_ref, gq), (gk_ref, gk), (gv_ref, gv))]
        return copies(pairs, out_sems, step)

    for step in range(TOKEN_STEPS):
        start(loads(step))
    for step in range(TOKEN_STEPS):
        wait(loads(step))
        for run in range(step * runs, (step + 1) * runs):
            rows = slice(run * group, (run + 1) * group)
            both = jnp.concatenate([tok[run, :, s].reshape(group * cuts, LANES) for s in range(2)], 1)
            out = dot(swap_ref[...], both)
            for j in range(cuts):
                lanes = slice(j * LANES, (j + 1) * LANES)
                conv = out[j * group : (j + 1) * group, :LANES]
                dgated = out[j * group : (j + 1) * group, LANES:]
                gq[rows, lanes] = (g[rows, lanes].astype(f32) * conv).astype(bf16)
                gk[rows, lanes] = (dgated * v[rows, lanes].astype(f32)).astype(bf16)
                gv[rows, lanes] = (dgated * k[rows, lanes].astype(f32)).astype(bf16)
        start(stores(step))
    for step in range(TOKEN_STEPS):
        wait(stores(step))


def finish(tok, key_in, value, grad_out):
    group = tok.shape[1] * tok.shape[3]
    channels, length = key_in.shape
    swap = jnp.asarray(swap_table(group))
    return pl.pallas_call(
        finish_kernel,
        in_specs=[ANY] * 4 + [VMEM],
        out_specs=[ANY] * 3,
        out_shape=[jax.ShapeDtypeStruct((channels, length), bf16)] * 3,
        scratch_shapes=[pltpu.VMEM(tok.shape, bf16)]
        + [pltpu.VMEM(key_in.shape, bf16)] * 6
        + [pltpu.SemaphoreType.DMA((TOKEN_STEPS, 4)), pltpu.SemaphoreType.DMA((TOKEN_STEPS, 3))],
        compiler_params=params(0, 52 * 2**20),
        cost_estimate=pl.CostEstimate(
            flops=3 * channels * length, bytes_accessed=16 * channels * length, transcendentals=0
        ),
        name="finish",
    )(tok, key_in, value, grad_out, swap)


def turned(stage, turn_cos, turn_sin, rows, at):
    lanes = slice(at * LANES, (at + 1) * LANES)
    re, im = stage[:rows, lanes], stage[rows:, lanes]
    return jnp.concatenate([re * turn_cos + im * turn_sin, im * turn_cos - re * turn_sin], 1)


def filter_kernel(x_ref, w_ref, m_ref, tc_ref, ts_ref, out_ref, *, scale):
    pair, rows, _ = x_ref.shape
    x = jnp.concatenate([x_ref[i] for i in range(pair)], 1)
    high = x.astype(bf16)
    low = (x - high.astype(f32)).astype(bf16)
    stage = dot(w_ref[...], jnp.concatenate([high, high, low], 0))
    for i in range(pair):
        u = turned(stage, tc_ref[...], ts_ref[...], rows, i) * scale
        u_high = u.astype(bf16)
        u_low = (u - u_high.astype(f32)).astype(bf16)
        out_ref[i] = dot(jnp.concatenate([u_high, u_high, u_low], 1), m_ref[...])


def filter_spectrum(filt, t, scale):
    n, rows, _ = filt.shape
    pair = FILTER_PAIR
    tables = [t["w3"], t["m3"], t["turn_cos"], t["turn_sin"]]
    return pl.pallas_call(
        functools.partial(filter_kernel, scale=scale),
        grid=(n // pair,),
        in_specs=[pl.BlockSpec((pair, rows, LANES), lambda i: (i, 0, 0))] + [whole(x) for x in tables],
        out_specs=pl.BlockSpec((pair, rows, 2 * LANES), lambda i: (i, 0, 0)),
        out_shape=jax.ShapeDtypeStruct((n, rows, 2 * LANES), f32),
        compiler_params=params(1),
        cost_estimate=pl.CostEstimate(
            flops=12 * n * rows * LANES * 512, bytes_accessed=16 * n * rows * LANES, transcendentals=0
        ),
        name="filter_spectrum",
    )(filt, *tables)


def back(spec, mi_ref, wi_ref, bc, bs, pair, rows):
    parts = mi_ref.shape[0] // (2 * LANES)
    stage = dot(jnp.concatenate([spec] * parts, 1), mi_ref[...])
    re_parts, im_parts = [], []
    for i in range(pair):
        re = stage[i * rows : (i + 1) * rows, :LANES]
        im = stage[i * rows : (i + 1) * rows, LANES:]
        re_parts.append((re * bc - im * bs).astype(bf16))
        im_parts.append((re * bs + im * bc).astype(bf16))
    v = jnp.concatenate([jnp.concatenate(re_parts, 1), jnp.concatenate(im_parts, 1)], 0)
    return dot(wi_ref[...], jnp.concatenate([v] * parts, 0))


def product(ar, ai, br, bi):
    return jnp.concatenate([ar * br - ai * bi, ar * bi + ai * br], 1)


def channels_kernel(
    x_ref, f_ref, w_hbm, m_hbm, tc_hbm, ts_hbm, mi_hbm, wi_hbm, cross_ref, out_ref,
    x_buf, f_buf, cross_buf, out_buf, w_ref, m_ref, tc_ref, ts_ref, mi_ref, wi_ref,
    in_sems, out_sems, table_sems, *, scale,
):
    n, split, _, kept, cuts, _ = x_ref.shape
    steps, count = f_buf.shape[:2]
    rows = n * cuts

    def loads(step):
        at = pl.ds(step * count, count)
        return copies([(x_ref.at[:, :, :, at], x_buf.at[step]), (f_ref.at[at], f_buf.at[step])], in_sems, step)

    def stores(step):
        at = pl.ds(step * count, count)
        return copies(
            [(cross_buf.at[step], cross_ref.at[at]), (out_buf.at[step], out_ref.at[:, :, :, at])], out_sems, step
        )

    tables = copies(
        [(w_hbm, w_ref), (tc_hbm, tc_ref), (ts_hbm, ts_ref), (m_hbm, m_ref), (mi_hbm, mi_ref), (wi_hbm, wi_ref)],
        table_sems, 0,
    )
    start(loads(0))
    start(tables)
    for step in range(1, steps):
        start(loads(step))
    wait(tables)

    @pl.loop(0, steps)
    def _(step):
        wait(loads(step))
        places = [(s, m, i) for s in range(2) for m in range(split) for i in range(count)]
        x = jnp.concatenate([x_buf[step, :, m, s, i].reshape(rows, LANES) for s, m, i in places], 1)
        stage = dot(w_ref[...], x)
        u = jnp.concatenate(
            [turned(stage, tc_ref[...], ts_ref[...], rows, i).astype(bf16) for i in range(len(places))], 0
        )
        spec = dot(u, m_ref[...])
        block = count * rows
        half = split * block
        f = f_buf[step].reshape(block, 2 * LANES)
        fr, fi = f[:, :LANES], f[:, LANES:]
        convs, dgateds, cross = [], [], 0.0
        for m in range(split):
            at = m * block
            gr, gi = spec[at : at + block, :LANES], spec[at : at + block, LANES:]
            dr, di = spec[half + at : half + at + block, :LANES], spec[half + at : half + at + block, LANES:]
            convs.append(product(fr, fi, gr, gi).astype(bf16))
            dgateds.append(product(fr, -fi, dr, di).astype(bf16))
            cross = cross + product(gr, -gi, dr, di)
        cross_buf[step] = (cross * scale).astype(bf16).reshape(count, rows, 2 * LANES)
        made = back(jnp.concatenate(convs + dgateds, 0), mi_ref, wi_ref, tc_ref[...], ts_ref[...], len(places), rows)
        made = made.astype(bf16)
        for at, (s, m, i) in enumerate(places):
            out_buf[step, :, m, s, i] = made[:, at * LANES : (at + 1) * LANES].reshape(n, cuts, LANES)
        start(stores(step))

    for step in range(steps):
        wait(stores(step))


def channels(x, f, t, scale):
    n, split, _, kept, cuts, _ = x.shape
    rows = n * cuts
    count = FILTERS
    steps = kept // count
    tables = [t[k] for k in ("w", "m", "turn_cos", "turn_sin", *TOKEN_BACK)]
    spec = (count, rows, 2 * LANES)
    block = (steps, n, split, 2, count, cuts, LANES)
    return pl.pallas_call(
        functools.partial(channels_kernel, scale=scale),
        in_specs=[ANY] * (2 + len(tables)),
        out_specs=[ANY] * 2,
        out_shape=[jax.ShapeDtypeStruct((kept, rows, 2 * LANES), bf16), jax.ShapeDtypeStruct(x.shape, bf16)],
        scratch_shapes=[
            pltpu.VMEM(block, bf16),
            pltpu.VMEM((steps, *spec), f32),
            pltpu.VMEM((steps, *spec), bf16),
            pltpu.VMEM(block, bf16),
            *[pltpu.VMEM(v.shape, v.dtype) for v in tables],
            pltpu.SemaphoreType.DMA((steps, 2)),
            pltpu.SemaphoreType.DMA((steps, 2)),
            pltpu.SemaphoreType.DMA((1, len(tables))),
        ],
        compiler_params=params(0),
        cost_estimate=pl.CostEstimate(
            flops=24 * split * kept * rows * LANES * 512, bytes_accessed=8 * x.size, transcendentals=0
        ),
        name="channels",
    )(x, f, *tables)


def lags_kernel(place_ref, spec_ref, mi_hbm, wi_hbm, tc_hbm, ts_hbm, *refs):
    *out_refs, spec, out_buf, mi_ref, wi_ref, tc_ref, ts_ref, in_sems, out_sems = refs
    ring, halves, kept, cuts, _ = out_buf.shape
    rows = spec.shape[1]
    moves = copies(
        [(spec_ref, spec), (mi_hbm, mi_ref), (tc_hbm, tc_ref), (ts_hbm, ts_ref), (wi_hbm, wi_ref)], in_sems, 0
    )
    start(moves)
    wait(moves)
    out = back(spec[...].reshape(kept * rows, 2 * LANES), mi_ref, wi_ref, tc_ref[...], ts_ref[...], kept, rows)
    out = out.astype(bf16)
    for place in range(ring * halves):
        at = place * cuts
        z, half = order(place, ring * halves)
        to = ((z - place_ref[0]) & (ring - 1), half ^ place_ref[1])
        for i in range(kept):
            out_buf[*to, i] = out[at : at + cuts, i * LANES : (i + 1) * LANES]
    moves = copies([(out_buf.at[z], out_refs[z]) for z in range(ring)], out_sems, 0)
    start(moves)
    wait(moves)


def lags(place, spec, t, n_tp, cuts):
    kept, rows, _ = spec.shape
    tables = [t[k] for k in (*CROSS_BACK, "turn_cos", "turn_sin")]
    ring = n_tp // SPLIT
    out = (SPLIT, kept, cuts, LANES)
    return pl.pallas_call(
        lags_kernel,
        in_specs=[pl.BlockSpec(memory_space=pltpu.SMEM)] + [ANY] * (1 + len(tables)),
        out_specs=[ANY] * ring,
        out_shape=[jax.ShapeDtypeStruct(out, bf16)] * ring,
        scratch_shapes=[
            pltpu.VMEM(spec.shape, bf16),
            pltpu.VMEM((ring, *out), bf16),
            *[pltpu.VMEM(v.shape, v.dtype) for v in tables],
            pltpu.SemaphoreType.DMA((1, 1 + len(tables))),
            pltpu.SemaphoreType.DMA((1, ring)),
        ],
        compiler_params=params(0),
        cost_estimate=pl.CostEstimate(
            flops=12 * kept * rows * LANES * 512, bytes_accessed=4 * spec.size, transcendentals=0
        ),
        name="lags",
    )(place, spec, *tables)


def order(place, n):
    return place % (n // SPLIT), place // (n // SPLIT)


def sum_scattered(parts, n):
    ring = n // SPLIT
    total = parts[0].astype(f32)
    for step in sorted(range(1, ring), key=lambda step: -min(step, ring - step)):
        pairs = [(i, i // ring * ring + (i + step) % ring) for i in range(n)]
        total = total + lax.ppermute(parts[step], "tp", pairs).astype(f32)
    return total


def body(query, key_in, value, grad_out, filter_raw, *, n_ctx, n_tp):
    group, length = filter_raw.shape
    rows = length // LANES
    kept = group // SPLIT
    root = 1.0 / math.sqrt(length)
    t = {k: jnp.asarray(v) for k, v in make_tables(length).items()}
    ring = n_tp // SPLIT
    sharing = [[c * n_tp + half * ring + z for c in range(n_ctx) for half in range(SPLIT)] for z in range(ring)]

    def exchange(x):
        flat = x.reshape(n_ctx * SPLIT, *x.shape[2:])
        flat = lax.all_to_all(
            flat, ("ctx", "tp"), split_axis=0, concat_axis=0, tiled=True, axis_index_groups=sharing
        )
        return flat.reshape(x.shape)

    place = order(lax.axis_index("tp"), n_tp)
    half = place[1]
    got = exchange(gate(query, key_in, value, grad_out, n_ctx))
    where = jnp.stack(place).astype(jnp.int32)
    filters = lax.dynamic_slice_in_dim(filter_raw, half * kept, kept, 0)
    filt = filter_spectrum(filters.reshape(kept, rows, LANES), t, root / length)
    filt, where = lax.optimization_barrier((filt, where))
    cross, made = channels(got, filt, t, root / length)
    tok = exchange(made)
    parts = lags(where, cross, t, n_tp, rows // n_ctx)
    total = sum_scattered(parts, n_tp)
    far = lax.ppermute(total[1], "tp", [(i, (i + ring) % n_tp) for i in range(n_tp)])
    grad_query, grad_key, grad_value = finish(tok, key_in, value, grad_out)
    mine, grad_query = lax.optimization_barrier((total[0], grad_query))
    first = jnp.where(half == 0, mine, far)
    second = jnp.where(half == 0, far, mine)
    filter_grad = jnp.concatenate([first, second], 0).reshape(group, length // n_tp)
    return (grad_query, grad_key, grad_value, filter_grad)


def solution(mesh):
    placed = (P("tp", "ctx"), P("tp", "ctx"), P("tp", "ctx"), P("tp", "ctx"), P("ctx", None))
    return jax.shard_map(
        functools.partial(body, n_ctx=mesh.shape["ctx"], n_tp=mesh.shape["tp"]),
        mesh=mesh,
        in_specs=placed,
        out_specs=(P("tp", "ctx"), P("tp", "ctx"), P("tp", "ctx"), P("ctx", "tp")),
        check_vma=False,
    )
```

```python
import functools
import math

import jax
import jax.numpy as jnp
import ml_dtypes
import numpy as np
from jax import lax
from jax.experimental import pallas as pl
from jax.experimental.pallas import tpu as pltpu
from jax.sharding import PartitionSpec as P

LANES = 128
VMEM_LIMIT = 56 * 2**20
SPLIT = 2
GATE_STEPS = 2
TOKEN_STEPS = 4
FILTERS = 4
FILTER_PAIR = 4
CROSS_BACK = ("mi", "wi")
TOKEN_BACK = ("mi", "wi")
f32 = jnp.float32
bf16 = jnp.bfloat16


def split_parts(table):
    high = table.astype(np.float32).astype(ml_dtypes.bfloat16)
    low = (table - high.astype(np.float64)).astype(np.float32).astype(ml_dtypes.bfloat16)
    return high, low


@functools.lru_cache(maxsize=None)
def make_tables(length):
    rows = length // LANES
    total = 2 * length
    a = np.arange(rows, dtype=np.float64)
    k1 = np.arange(rows, dtype=np.float64) + 0.5
    b = np.arange(LANES, dtype=np.float64)
    first = 2.0 * np.pi * np.outer(k1, a) / (2 * rows)
    turn = 2.0 * np.pi * np.outer(k1, b) / total
    second = 2.0 * np.pi * np.outer(b, b) / LANES
    c2, s2 = np.cos(second), np.sin(second)
    w_high, w_low = split_parts(np.concatenate([np.cos(first), -np.sin(first)], 0))
    m_high, m_low = split_parts(np.block([[c2, -s2], [s2, c2]]))
    mi_high, mi_low = split_parts(np.block([[c2, s2], [-s2, c2]]))
    wi_high, wi_low = split_parts(np.concatenate([np.cos(first).T, -np.sin(first).T], 1))
    return dict(
        w3=np.concatenate([w_high, w_low, w_high], 1),
        m3=np.concatenate([m_high, m_low, m_high], 0),
        w=w_high,
        m=m_high,
        mi=mi_high,
        wi=wi_high,
        mi2=np.concatenate([mi_high, mi_low], 0),
        wi2=np.concatenate([wi_high, wi_low], 1),
        turn_cos=np.cos(turn).astype(np.float32),
        turn_sin=np.sin(turn).astype(np.float32),
    )


def dot(x, y):
    return jnp.dot(x, y, preferred_element_type=f32)


def whole(table):
    return pl.BlockSpec(table.shape, lambda *_: (0,) * table.ndim)


def params(grid_rank, limit=VMEM_LIMIT):
    return pltpu.CompilerParams(
        dimension_semantics=("arbitrary",) * grid_rank if grid_rank else None,
        vmem_limit_bytes=limit,
    )


def swap_table(size):
    index = np.arange(size * size).reshape(size, size)
    table = np.zeros((size * size, size * size), np.float32)
    table[index.T.reshape(-1), index.reshape(-1)] = 1.0
    return table.astype(ml_dtypes.bfloat16)


def copies(pairs, sems, at):
    return [pltpu.make_async_copy(src, dst, sems.at[at, i]) for i, (src, dst) in enumerate(pairs)]


def start(moves):
    for move in moves:
        move.start()


def wait(moves):
    for move in moves:
        move.wait()


ANY = pl.BlockSpec(memory_space=pl.ANY)
VMEM = pl.BlockSpec(memory_space=pltpu.VMEM)


def gate_kernel(
    q_ref, k_ref, v_ref, g_ref, swap_hbm, out_ref, q, k, v, g, o, swap_ref, in_sems, out_sems, swap_sems
):
    n, split, _, kept, cuts, _ = out_ref.shape
    group = split * kept
    runs = n // GATE_STEPS

    def loads(step):
        rows = pl.ds(step * runs * group, runs * group)
        pairs = [(r.at[rows], s.at[rows]) for r, s in ((k_ref, k), (v_ref, v), (g_ref, g), (q_ref, q))]
        return copies(pairs, in_sems, step)

    def stores(step):
        at = pl.ds(step * runs, runs)
        return copies([(o.at[at], out_ref.at[at])], out_sems, step)

    swap = copies([(swap_hbm, swap_ref)], swap_sems, 0)
    start(swap)
    for step in range(GATE_STEPS):
        start(loads(step))
    wait(swap)
    for step in range(GATE_STEPS):
        wait(loads(step))
        for run in range(step * runs, (step + 1) * runs):
            rows = slice(run * group, (run + 1) * group)

            def product(x, y):
                z = x[rows, :] * y[rows, :]
                return jnp.concatenate([z[:, j * LANES : (j + 1) * LANES] for j in range(cuts)], 0)

            both = jnp.concatenate([product(k, v), product(g, q)], 1)
            out = dot(swap_ref[...], both).astype(bf16)
            for s in range(2):
                o[run, :, s] = out[:, s * LANES : (s + 1) * LANES].reshape(split, kept, cuts, LANES)
        start(stores(step))
    for step in range(GATE_STEPS):
        wait(stores(step))


def gate(query, key_in, value, grad_out, n):
    channels, length = query.shape
    group = channels // n
    cuts = length // LANES
    swap = jnp.asarray(swap_table(group))
    sent = (n, SPLIT, 2, group // SPLIT, cuts, LANES)
    return pl.pallas_call(
        gate_kernel,
        in_specs=[ANY] * 5,
        out_specs=ANY,
        out_shape=jax.ShapeDtypeStruct(sent, bf16),
        scratch_shapes=[pltpu.VMEM(query.shape, bf16)] * 4
        + [
            pltpu.VMEM(sent, bf16),
            pltpu.VMEM(swap.shape, bf16),
            pltpu.SemaphoreType.DMA((GATE_STEPS, 4)),
            pltpu.SemaphoreType.DMA((GATE_STEPS, 1)),
            pltpu.SemaphoreType.DMA((1, 1)),
        ],
        compiler_params=params(0),
        cost_estimate=pl.CostEstimate(
            flops=2 * channels * length, bytes_accessed=12 * channels * length, transcendentals=0
        ),
        name="gate",
    )(query, key_in, value, grad_out, swap)


def finish_kernel(
    tok_ref, k_ref, v_ref, g_ref, swap_ref, gq_ref, gk_ref, gv_ref, tok, k, v, g, gq, gk, gv, in_sems, out_sems
):
    n, split, _, kept, cuts, _ = tok_ref.shape
    group = split * kept
    runs = n // TOKEN_STEPS

    def loads(step):
        rows = pl.ds(step * runs * group, runs * group)
        at = pl.ds(step * runs, runs)
        pairs = [(tok_ref.at[at], tok.at[at])]
        pairs += [(r.at[rows], s.at[rows]) for r, s in ((g_ref, g), (v_ref, v), (k_ref, k))]
        return copies(pairs, in_sems, step)

    def stores(step):
        rows = pl.ds(step * runs * group, runs * group)
        pairs = [(s.at[rows], r.at[rows]) for r, s in ((gq_ref, gq), (gk_ref, gk), (gv_ref, gv))]
        return copies(pairs, out_sems, step)

    for step in range(TOKEN_STEPS):
        start(loads(step))
    for step in range(TOKEN_STEPS):
        wait(loads(step))
        for run in range(step * runs, (step + 1) * runs):
            rows = slice(run * group, (run + 1) * group)
            both = jnp.concatenate([tok[run, :, s].reshape(group * cuts, LANES) for s in range(2)], 1)
            out = dot(swap_ref[...], both).astype(bf16)
            for j in range(cuts):
                lanes = slice(j * LANES, (j + 1) * LANES)
                conv = out[j * group : (j + 1) * group, :LANES]
                dgated = out[j * group : (j + 1) * group, LANES:]
                gq[rows, lanes] = g[rows, lanes] * conv
                gk[rows, lanes] = dgated * v[rows, lanes]
                gv[rows, lanes] = dgated * k[rows, lanes]
        start(stores(step))
    for step in range(TOKEN_STEPS):
        wait(stores(step))


def finish(tok, key_in, value, grad_out):
    group = tok.shape[1] * tok.shape[3]
    channels, length = key_in.shape
    swap = jnp.asarray(swap_table(group))
    return pl.pallas_call(
        finish_kernel,
        in_specs=[ANY] * 4 + [VMEM],
        out_specs=[ANY] * 3,
        out_shape=[jax.ShapeDtypeStruct((channels, length), bf16)] * 3,
        scratch_shapes=[pltpu.VMEM(tok.shape, bf16)]
        + [pltpu.VMEM(key_in.shape, bf16)] * 6
        + [pltpu.SemaphoreType.DMA((TOKEN_STEPS, 4)), pltpu.SemaphoreType.DMA((TOKEN_STEPS, 3))],
        compiler_params=params(0, 52 * 2**20),
        cost_estimate=pl.CostEstimate(
            flops=3 * channels * length, bytes_accessed=16 * channels * length, transcendentals=0
        ),
        name="finish",
    )(tok, key_in, value, grad_out, swap)


def turned(stage, turn_cos, turn_sin, rows, at):
    lanes = slice(at * LANES, (at + 1) * LANES)
    re, im = stage[:rows, lanes], stage[rows:, lanes]
    return jnp.concatenate([re * turn_cos + im * turn_sin, im * turn_cos - re * turn_sin], 1)


def filter_kernel(x_ref, w_ref, m_ref, tc_ref, ts_ref, out_ref, *, scale):
    pair, rows, _ = x_ref.shape
    x = jnp.concatenate([x_ref[i] for i in range(pair)], 1)
    high = x.astype(bf16)
    low = (x - high.astype(f32)).astype(bf16)
    stage = dot(w_ref[...], jnp.concatenate([high, high, low], 0))
    for i in range(pair):
        u = turned(stage, tc_ref[...], ts_ref[...], rows, i) * scale
        u_high = u.astype(bf16)
        u_low = (u - u_high.astype(f32)).astype(bf16)
        out_ref[i] = dot(jnp.concatenate([u_high, u_high, u_low], 1), m_ref[...])


def filter_spectrum(filt, t, scale):
    n, rows, _ = filt.shape
    pair = FILTER_PAIR
    tables = [t["w3"], t["m3"], t["turn_cos"], t["turn_sin"]]
    return pl.pallas_call(
        functools.partial(filter_kernel, scale=scale),
        grid=(n // pair,),
        in_specs=[pl.BlockSpec((pair, rows, LANES), lambda i: (i, 0, 0))] + [whole(x) for x in tables],
        out_specs=pl.BlockSpec((pair, rows, 2 * LANES), lambda i: (i, 0, 0)),
        out_shape=jax.ShapeDtypeStruct((n, rows, 2 * LANES), f32),
        compiler_params=params(1),
        cost_estimate=pl.CostEstimate(
            flops=12 * n * rows * LANES * 512, bytes_accessed=16 * n * rows * LANES, transcendentals=0
        ),
        name="filter_spectrum",
    )(filt, *tables)


def back(spec, mi_ref, wi_ref, bc, bs, pair, rows):
    parts = mi_ref.shape[0] // (2 * LANES)
    stage = dot(jnp.concatenate([spec] * parts, 1), mi_ref[...])
    re_parts, im_parts = [], []
    for i in range(pair):
        re = stage[i * rows : (i + 1) * rows, :LANES]
        im = stage[i * rows : (i + 1) * rows, LANES:]
        re_parts.append((re * bc - im * bs).astype(bf16))
        im_parts.append((re * bs + im * bc).astype(bf16))
    v = jnp.concatenate([jnp.concatenate(re_parts, 1), jnp.concatenate(im_parts, 1)], 0)
    return dot(wi_ref[...], jnp.concatenate([v] * parts, 0))


def product(ar, ai, br, bi):
    return jnp.concatenate([ar * br - ai * bi, ar * bi + ai * br], 1)


def channels_kernel(
    x_ref, f_ref, w_hbm, m_hbm, tc_hbm, ts_hbm, mi_hbm, wi_hbm, cross_ref, out_ref,
    x_buf, f_buf, cross_buf, out_buf, w_ref, m_ref, tc_ref, ts_ref, mi_ref, wi_ref,
    in_sems, out_sems, table_sems, *, scale,
):
    n, split, _, kept, cuts, _ = x_ref.shape
    steps, count = f_buf.shape[:2]
    rows = n * cuts

    def loads(step):
        at = pl.ds(step * count, count)
        return copies([(x_ref.at[:, :, :, at], x_buf.at[step]), (f_ref.at[at], f_buf.at[step])], in_sems, step)

    def stores(step):
        at = pl.ds(step * count, count)
        return copies(
            [(cross_buf.at[step], cross_ref.at[at]), (out_buf.at[step], out_ref.at[:, :, :, at])], out_sems, step
        )

    tables = copies(
        [(w_hbm, w_ref), (tc_hbm, tc_ref), (ts_hbm, ts_ref), (m_hbm, m_ref), (mi_hbm, mi_ref), (wi_hbm, wi_ref)],
        table_sems, 0,
    )
    start(loads(0))
    start(tables)
    for step in range(1, steps):
        start(loads(step))
    wait(tables)

    @pl.loop(0, steps)
    def _(step):
        wait(loads(step))
        places = [(s, m, i) for s in range(2) for m in range(split) for i in range(count)]
        x = jnp.concatenate([x_buf[step, :, m, s, i].reshape(rows, LANES) for s, m, i in places], 1)
        stage = dot(w_ref[...], x)
        u = jnp.concatenate(
            [turned(stage, tc_ref[...], ts_ref[...], rows, i).astype(bf16) for i in range(len(places))], 0
        )
        spec = dot(u, m_ref[...])
        block = count * rows
        half = split * block
        f = f_buf[step].reshape(block, 2 * LANES)
        fr, fi = f[:, :LANES], f[:, LANES:]
        convs, dgateds, cross = [], [], 0.0
        for m in range(split):
            at = m * block
            gr, gi = spec[at : at + block, :LANES], spec[at : at + block, LANES:]
            dr, di = spec[half + at : half + at + block, :LANES], spec[half + at : half + at + block, LANES:]
            convs.append(product(fr, fi, gr, gi).astype(bf16))
            dgateds.append(product(fr, -fi, dr, di).astype(bf16))
            cross = cross + product(gr, -gi, dr, di)
        cross_buf[step] = (cross * scale).astype(bf16).reshape(count, rows, 2 * LANES)
        made = back(jnp.concatenate(convs + dgateds, 0), mi_ref, wi_ref, tc_ref[...], ts_ref[...], len(places), rows)
        made = made.astype(bf16)
        for at, (s, m, i) in enumerate(places):
            out_buf[step, :, m, s, i] = made[:, at * LANES : (at + 1) * LANES].reshape(n, cuts, LANES)
        start(stores(step))

    for step in range(steps):
        wait(stores(step))


def channels(x, f, t, scale):
    n, split, _, kept, cuts, _ = x.shape
    rows = n * cuts
    count = FILTERS
    steps = kept // count
    tables = [t[k] for k in ("w", "m", "turn_cos", "turn_sin", *TOKEN_BACK)]
    spec = (count, rows, 2 * LANES)
    block = (steps, n, split, 2, count, cuts, LANES)
    return pl.pallas_call(
        functools.partial(channels_kernel, scale=scale),
        in_specs=[ANY] * (2 + len(tables)),
        out_specs=[ANY] * 2,
        out_shape=[jax.ShapeDtypeStruct((kept, rows, 2 * LANES), bf16), jax.ShapeDtypeStruct(x.shape, bf16)],
        scratch_shapes=[
            pltpu.VMEM(block, bf16),
            pltpu.VMEM((steps, *spec), f32),
            pltpu.VMEM((steps, *spec), bf16),
            pltpu.VMEM(block, bf16),
            *[pltpu.VMEM(v.shape, v.dtype) for v in tables],
            pltpu.SemaphoreType.DMA((steps, 2)),
            pltpu.SemaphoreType.DMA((steps, 2)),
            pltpu.SemaphoreType.DMA((1, len(tables))),
        ],
        compiler_params=params(0),
        cost_estimate=pl.CostEstimate(
            flops=24 * split * kept * rows * LANES * 512, bytes_accessed=8 * x.size, transcendentals=0
        ),
        name="channels",
    )(x, f, *tables)


def lags_kernel(place_ref, spec_ref, mi_hbm, wi_hbm, tc_hbm, ts_hbm, *refs):
    *out_refs, spec, out_buf, mi_ref, wi_ref, tc_ref, ts_ref, in_sems, out_sems = refs
    ring, halves, kept, cuts, _ = out_buf.shape
    rows = spec.shape[1]
    moves = copies(
        [(spec_ref, spec), (mi_hbm, mi_ref), (tc_hbm, tc_ref), (ts_hbm, ts_ref), (wi_hbm, wi_ref)], in_sems, 0
    )
    start(moves)
    wait(moves)
    out = back(spec[...].reshape(kept * rows, 2 * LANES), mi_ref, wi_ref, tc_ref[...], ts_ref[...], kept, rows)
    out = out.astype(bf16)
    for place in range(ring * halves):
        at = place * cuts
        z, half = order(place, ring * halves)
        to = ((z - place_ref[0]) & (ring - 1), half ^ place_ref[1])
        for i in range(kept):
            out_buf[*to, i] = out[at : at + cuts, i * LANES : (i + 1) * LANES]
    moves = copies([(out_buf.at[z], out_refs[z]) for z in range(ring)], out_sems, 0)
    start(moves)
    wait(moves)


def lags(place, spec, t, n_tp, cuts):
    kept, rows, _ = spec.shape
    tables = [t[k] for k in (*CROSS_BACK, "turn_cos", "turn_sin")]
    ring = n_tp // SPLIT
    out = (SPLIT, kept, cuts, LANES)
    return pl.pallas_call(
        lags_kernel,
        in_specs=[pl.BlockSpec(memory_space=pltpu.SMEM)] + [ANY] * (1 + len(tables)),
        out_specs=[ANY] * ring,
        out_shape=[jax.ShapeDtypeStruct(out, bf16)] * ring,
        scratch_shapes=[
            pltpu.VMEM(spec.shape, bf16),
            pltpu.VMEM((ring, *out), bf16),
            *[pltpu.VMEM(v.shape, v.dtype) for v in tables],
            pltpu.SemaphoreType.DMA((1, 1 + len(tables))),
            pltpu.SemaphoreType.DMA((1, ring)),
        ],
        compiler_params=params(0),
        cost_estimate=pl.CostEstimate(
            flops=12 * kept * rows * LANES * 512, bytes_accessed=4 * spec.size, transcendentals=0
        ),
        name="lags",
    )(place, spec, *tables)


def order(place, n):
    return place % (n // SPLIT), place // (n // SPLIT)


def sum_scattered(parts, n):
    ring = n // SPLIT
    total = parts[0].astype(f32)
    for step in sorted(range(1, ring), key=lambda step: -min(step, ring - step)):
        pairs = [(i, i // ring * ring + (i + step) % ring) for i in range(n)]
        total = total + lax.ppermute(parts[step], "tp", pairs).astype(f32)
    return total


def body(query, key_in, value, grad_out, filter_raw, *, n_ctx, n_tp):
    group, length = filter_raw.shape
    rows = length // LANES
    kept = group // SPLIT
    root = 1.0 / math.sqrt(length)
    t = {k: jnp.asarray(v) for k, v in make_tables(length).items()}
    ring = n_tp // SPLIT
    sharing = [[c * n_tp + half * ring + z for c in range(n_ctx) for half in range(SPLIT)] for z in range(ring)]

    def exchange(x):
        flat = x.reshape(n_ctx * SPLIT, *x.shape[2:])
        flat = lax.all_to_all(
            flat, ("ctx", "tp"), split_axis=0, concat_axis=0, tiled=True, axis_index_groups=sharing
        )
        return flat.reshape(x.shape)

    place = order(lax.axis_index("tp"), n_tp)
    half = place[1]
    got = exchange(gate(query, key_in, value, grad_out, n_ctx))
    where = jnp.stack(place).astype(jnp.int32)
    filters = lax.dynamic_slice_in_dim(filter_raw, half * kept, kept, 0)
    filt = filter_spectrum(filters.reshape(kept, rows, LANES), t, root / length)
    filt, where = lax.optimization_barrier((filt, where))
    cross, made = channels(got, filt, t, root / length)
    tok = exchange(made)
    parts = lags(where, cross, t, n_tp, rows // n_ctx)
    total = sum_scattered(parts, n_tp)
    total = total.reshape(SPLIT, kept, length // n_tp)
    far = lax.ppermute(total[1], "tp", [(i, (i + ring) % n_tp) for i in range(n_tp)])
    grad_query, grad_key, grad_value = finish(tok, key_in, value, grad_out)
    mine, grad_query = lax.optimization_barrier((total[0], grad_query))
    filter_grad = jnp.where(jnp.arange(SPLIT)[:, None, None] == half, mine, far).reshape(group, length // n_tp)
    return (grad_query, grad_key, grad_value, filter_grad)


def solution(mesh):
    placed = (P("tp", "ctx"), P("tp", "ctx"), P("tp", "ctx"), P("tp", "ctx"), P("ctx", None))
    return jax.shard_map(
        functools.partial(body, n_ctx=mesh.shape["ctx"], n_tp=mesh.shape["tp"]),
        mesh=mesh,
        in_specs=placed,
        out_specs=(P("tp", "ctx"), P("tp", "ctx"), P("tp", "ctx"), P("ctx", "tp")),
        check_vma=False,
    )
```

```python
import functools
import math

import jax
import jax.numpy as jnp
import ml_dtypes
import numpy as np
from jax import lax
from jax.experimental import pallas as pl
from jax.experimental.pallas import tpu as pltpu
from jax.sharding import PartitionSpec as P

LANES = 128
VMEM_LIMIT = 56 * 2**20
SPLIT = 2
GATE_STEPS = 2
TOKEN_STEPS = 4
FILTERS = 4
FILTER_PAIR = 4
CROSS_BACK = ("mi", "wi")
TOKEN_BACK = ("mi", "wi")
f32 = jnp.float32
bf16 = jnp.bfloat16


def split_parts(table):
    high = table.astype(np.float32).astype(ml_dtypes.bfloat16)
    low = (table - high.astype(np.float64)).astype(np.float32).astype(ml_dtypes.bfloat16)
    return high, low


@functools.lru_cache(maxsize=None)
def make_tables(length):
    rows = length // LANES
    total = 2 * length
    a = np.arange(rows, dtype=np.float64)
    k1 = np.arange(rows, dtype=np.float64) + 0.5
    b = np.arange(LANES, dtype=np.float64)
    first = 2.0 * np.pi * np.outer(k1, a) / (2 * rows)
    turn = 2.0 * np.pi * np.outer(k1, b) / total
    second = 2.0 * np.pi * np.outer(b, b) / LANES
    c2, s2 = np.cos(second), np.sin(second)
    w_high, w_low = split_parts(np.concatenate([np.cos(first), -np.sin(first)], 0))
    m_high, m_low = split_parts(np.block([[c2, -s2], [s2, c2]]))
    mi_high, mi_low = split_parts(np.block([[c2, s2], [-s2, c2]]))
    wi_high, wi_low = split_parts(np.concatenate([np.cos(first).T, -np.sin(first).T], 1))
    return dict(
        w3=np.concatenate([w_high, w_low, w_high], 1),
        m3=np.concatenate([m_high, m_low, m_high], 0),
        w=w_high,
        m=m_high,
        mi=mi_high,
        wi=wi_high,
        mi2=np.concatenate([mi_high, mi_low], 0),
        wi2=np.concatenate([wi_high, wi_low], 1),
        turn_cos=np.cos(turn).astype(np.float32),
        turn_sin=np.sin(turn).astype(np.float32),
    )


def dot(x, y):
    return jnp.dot(x, y, preferred_element_type=f32)


def whole(table):
    return pl.BlockSpec(table.shape, lambda *_: (0,) * table.ndim)


def params(grid_rank, limit=VMEM_LIMIT):
    return pltpu.CompilerParams(
        dimension_semantics=("arbitrary",) * grid_rank if grid_rank else None,
        vmem_limit_bytes=limit,
    )


def swap_table(size):
    index = np.arange(size * size).reshape(size, size)
    table = np.zeros((size * size, size * size), np.float32)
    table[index.T.reshape(-1), index.reshape(-1)] = 1.0
    return table.astype(ml_dtypes.bfloat16)


def copies(pairs, sems, at):
    return [pltpu.make_async_copy(src, dst, sems.at[at, i]) for i, (src, dst) in enumerate(pairs)]


def start(moves):
    for move in moves:
        move.start()


def wait(moves):
    for move in moves:
        move.wait()


ANY = pl.BlockSpec(memory_space=pl.ANY)
VMEM = pl.BlockSpec(memory_space=pltpu.VMEM)


def gate_kernel(
    q_ref, k_ref, v_ref, g_ref, swap_hbm, out_ref, q, k, v, g, o, swap_ref, in_sems, out_sems, swap_sems
):
    n, split, _, kept, cuts, _ = out_ref.shape
    group = split * kept
    runs = n // GATE_STEPS

    def loads(step):
        rows = pl.ds(step * runs * group, runs * group)
        pairs = [(r.at[rows], s.at[rows]) for r, s in ((k_ref, k), (v_ref, v), (g_ref, g), (q_ref, q))]
        return copies(pairs, in_sems, step)

    def stores(step):
        at = pl.ds(step * runs, runs)
        return copies([(o.at[at], out_ref.at[at])], out_sems, step)

    swap = copies([(swap_hbm, swap_ref)], swap_sems, 0)
    start(swap)
    for step in range(GATE_STEPS):
        start(loads(step))
    wait(swap)
    for step in range(GATE_STEPS):
        wait(loads(step))
        for run in range(step * runs, (step + 1) * runs):
            rows = slice(run * group, (run + 1) * group)

            def product(x, y):
                z = x[rows, :] * y[rows, :]
                return jnp.concatenate([z[:, j * LANES : (j + 1) * LANES] for j in range(cuts)], 0)

            both = jnp.concatenate([product(k, v), product(g, q)], 1)
            out = dot(swap_ref[...], both).astype(bf16)
            for s in range(2):
                o[run, :, s] = out[:, s * LANES : (s + 1) * LANES].reshape(split, kept, cuts, LANES)
        start(stores(step))
    for step in range(GATE_STEPS):
        wait(stores(step))


def gate(query, key_in, value, grad_out, n):
    channels, length = query.shape
    group = channels // n
    cuts = length // LANES
    swap = jnp.asarray(swap_table(group))
    sent = (n, SPLIT, 2, group // SPLIT, cuts, LANES)
    return pl.pallas_call(
        gate_kernel,
        in_specs=[ANY] * 5,
        out_specs=ANY,
        out_shape=jax.ShapeDtypeStruct(sent, bf16),
        scratch_shapes=[pltpu.VMEM(query.shape, bf16)] * 4
        + [
            pltpu.VMEM(sent, bf16),
            pltpu.VMEM(swap.shape, bf16),
            pltpu.SemaphoreType.DMA((GATE_STEPS, 4)),
            pltpu.SemaphoreType.DMA((GATE_STEPS, 1)),
            pltpu.SemaphoreType.DMA((1, 1)),
        ],
        compiler_params=params(0),
        cost_estimate=pl.CostEstimate(
            flops=2 * channels * length, bytes_accessed=12 * channels * length, transcendentals=0
        ),
        name="gate",
    )(query, key_in, value, grad_out, swap)


def finish_kernel(
    tok_ref, k_ref, v_ref, g_ref, swap_ref, gq_ref, gk_ref, gv_ref, tok, k, v, g, gq, gk, gv, in_sems, out_sems
):
    n, split, _, kept, cuts, _ = tok_ref.shape
    group = split * kept
    runs = n // TOKEN_STEPS

    def loads(step):
        rows = pl.ds(step * runs * group, runs * group)
        at = pl.ds(step * runs, runs)
        pairs = [(tok_ref.at[at], tok.at[at])]
        pairs += [(r.at[rows], s.at[rows]) for r, s in ((g_ref, g), (v_ref, v), (k_ref, k))]
        return copies(pairs, in_sems, step)

    def stores(step):
        rows = pl.ds(step * runs * group, runs * group)
        pairs = [(s.at[rows], r.at[rows]) for r, s in ((gq_ref, gq), (gk_ref, gk), (gv_ref, gv))]
        return copies(pairs, out_sems, step)

    for step in range(TOKEN_STEPS):
        start(loads(step))
    for step in range(TOKEN_STEPS):
        wait(loads(step))
        for run in range(step * runs, (step + 1) * runs):
            rows = slice(run * group, (run + 1) * group)
            both = jnp.concatenate([tok[run, :, s].reshape(group * cuts, LANES) for s in range(2)], 1)
            out = dot(swap_ref[...], both).astype(bf16)
            for j in range(cuts):
                lanes = slice(j * LANES, (j + 1) * LANES)
                conv = out[j * group : (j + 1) * group, :LANES]
                dgated = out[j * group : (j + 1) * group, LANES:]
                gq[rows, lanes] = g[rows, lanes] * conv
                gk[rows, lanes] = dgated * v[rows, lanes]
                gv[rows, lanes] = dgated * k[rows, lanes]
        start(stores(step))
    for step in range(TOKEN_STEPS):
        wait(stores(step))


def finish(tok, key_in, value, grad_out):
    group = tok.shape[1] * tok.shape[3]
    channels, length = key_in.shape
    swap = jnp.asarray(swap_table(group))
    return pl.pallas_call(
        finish_kernel,
        in_specs=[ANY] * 4 + [VMEM],
        out_specs=[ANY] * 3,
        out_shape=[jax.ShapeDtypeStruct((channels, length), bf16)] * 3,
        scratch_shapes=[pltpu.VMEM(tok.shape, bf16)]
        + [pltpu.VMEM(key_in.shape, bf16)] * 6
        + [pltpu.SemaphoreType.DMA((TOKEN_STEPS, 4)), pltpu.SemaphoreType.DMA((TOKEN_STEPS, 3))],
        compiler_params=params(0, 52 * 2**20),
        cost_estimate=pl.CostEstimate(
            flops=3 * channels * length, bytes_accessed=16 * channels * length, transcendentals=0
        ),
        name="finish",
    )(tok, key_in, value, grad_out, swap)


def turned(stage, turn_cos, turn_sin, rows, at):
    lanes = slice(at * LANES, (at + 1) * LANES)
    re, im = stage[:rows, lanes], stage[rows:, lanes]
    return jnp.concatenate([re * turn_cos + im * turn_sin, im * turn_cos - re * turn_sin], 1)


def filter_kernel(x_ref, w_ref, m_ref, tc_ref, ts_ref, out_ref, *, scale):
    pair, rows, _ = x_ref.shape
    x = jnp.concatenate([x_ref[i] for i in range(pair)], 1)
    high = x.astype(bf16)
    low = (x - high.astype(f32)).astype(bf16)
    stage = dot(w_ref[...], jnp.concatenate([high, high, low], 0))
    for i in range(pair):
        u = turned(stage, tc_ref[...], ts_ref[...], rows, i) * scale
        u_high = u.astype(bf16)
        u_low = (u - u_high.astype(f32)).astype(bf16)
        out_ref[i] = dot(jnp.concatenate([u_high, u_high, u_low], 1), m_ref[...])


def filter_spectrum(filt, t, scale):
    n, rows, _ = filt.shape
    pair = FILTER_PAIR
    tables = [t["w3"], t["m3"], t["turn_cos"], t["turn_sin"]]
    return pl.pallas_call(
        functools.partial(filter_kernel, scale=scale),
        grid=(n // pair,),
        in_specs=[pl.BlockSpec((pair, rows, LANES), lambda i: (i, 0, 0))] + [whole(x) for x in tables],
        out_specs=pl.BlockSpec((pair, rows, 2 * LANES), lambda i: (i, 0, 0)),
        out_shape=jax.ShapeDtypeStruct((n, rows, 2 * LANES), f32),
        compiler_params=params(1),
        cost_estimate=pl.CostEstimate(
            flops=12 * n * rows * LANES * 512, bytes_accessed=16 * n * rows * LANES, transcendentals=0
        ),
        name="filter_spectrum",
    )(filt, *tables)


def back(spec, mi_ref, wi_ref, bc, bs, pair, rows):
    parts = mi_ref.shape[0] // (2 * LANES)
    stage = dot(jnp.concatenate([spec] * parts, 1), mi_ref[...])
    re_parts, im_parts = [], []
    for i in range(pair):
        re = stage[i * rows : (i + 1) * rows, :LANES]
        im = stage[i * rows : (i + 1) * rows, LANES:]
        re_parts.append((re * bc - im * bs).astype(bf16))
        im_parts.append((re * bs + im * bc).astype(bf16))
    v = jnp.concatenate([jnp.concatenate(re_parts, 1), jnp.concatenate(im_parts, 1)], 0)
    return dot(wi_ref[...], jnp.concatenate([v] * parts, 0))


def product(ar, ai, br, bi):
    return jnp.concatenate([ar * br - ai * bi, ar * bi + ai * br], 1)


def channels_kernel(
    x_ref, f_ref, w_hbm, m_hbm, tc_hbm, ts_hbm, mi_hbm, wi_hbm, cross_ref, out_ref,
    x_buf, f_buf, cross_buf, out_buf, w_ref, m_ref, tc_ref, ts_ref, mi_ref, wi_ref,
    in_sems, out_sems, table_sems, *, scale,
):
    n, split, _, kept, cuts, _ = x_ref.shape
    steps, count = f_buf.shape[:2]
    rows = n * cuts

    def loads(step):
        at = pl.ds(step * count, count)
        return copies([(x_ref.at[:, :, :, at], x_buf.at[step]), (f_ref.at[at], f_buf.at[step])], in_sems, step)

    def stores(step):
        at = pl.ds(step * count, count)
        return copies(
            [(cross_buf.at[step], cross_ref.at[at]), (out_buf.at[step], out_ref.at[:, :, :, at])], out_sems, step
        )

    tables = copies(
        [(w_hbm, w_ref), (tc_hbm, tc_ref), (ts_hbm, ts_ref), (m_hbm, m_ref), (mi_hbm, mi_ref), (wi_hbm, wi_ref)],
        table_sems, 0,
    )
    start(loads(0))
    start(tables)
    for step in range(1, steps):
        start(loads(step))
    wait(tables)

    @pl.loop(0, steps)
    def _(step):
        wait(loads(step))
        places = [(s, m, i) for s in range(2) for m in range(split) for i in range(count)]
        x = jnp.concatenate([x_buf[step, :, m, s, i].reshape(rows, LANES) for s, m, i in places], 1)
        stage = dot(w_ref[...], x)
        u = jnp.concatenate(
            [turned(stage, tc_ref[...], ts_ref[...], rows, i).astype(bf16) for i in range(len(places))], 0
        )
        spec = dot(u, m_ref[...])
        block = count * rows
        half = split * block
        f = f_buf[step].reshape(block, 2 * LANES)
        fr, fi = f[:, :LANES], f[:, LANES:]
        convs, dgateds, cross = [], [], 0.0
        for m in range(split):
            at = m * block
            gr, gi = spec[at : at + block, :LANES], spec[at : at + block, LANES:]
            dr, di = spec[half + at : half + at + block, :LANES], spec[half + at : half + at + block, LANES:]
            convs.append(product(fr, fi, gr, gi).astype(bf16))
            dgateds.append(product(fr, -fi, dr, di).astype(bf16))
            cross = cross + product(gr, -gi, dr, di)
        cross_buf[step] = (cross * scale).astype(bf16).reshape(count, rows, 2 * LANES)
        made = back(jnp.concatenate(convs + dgateds, 0), mi_ref, wi_ref, tc_ref[...], ts_ref[...], len(places), rows)
        made = made.astype(bf16)
        for at, (s, m, i) in enumerate(places):
            out_buf[step, :, m, s, i] = made[:, at * LANES : (at + 1) * LANES].reshape(n, cuts, LANES)
        start(stores(step))

    for step in range(steps):
        wait(stores(step))


def channels(x, f, t, scale):
    n, split, _, kept, cuts, _ = x.shape
    rows = n * cuts
    count = FILTERS
    steps = kept // count
    tables = [t[k] for k in ("w", "m", "turn_cos", "turn_sin", *TOKEN_BACK)]
    spec = (count, rows, 2 * LANES)
    block = (steps, n, split, 2, count, cuts, LANES)
    return pl.pallas_call(
        functools.partial(channels_kernel, scale=scale),
        in_specs=[ANY] * (2 + len(tables)),
        out_specs=[ANY] * 2,
        out_shape=[jax.ShapeDtypeStruct((kept, rows, 2 * LANES), bf16), jax.ShapeDtypeStruct(x.shape, bf16)],
        scratch_shapes=[
            pltpu.VMEM(block, bf16),
            pltpu.VMEM((steps, *spec), f32),
            pltpu.VMEM((steps, *spec), bf16),
            pltpu.VMEM(block, bf16),
            *[pltpu.VMEM(v.shape, v.dtype) for v in tables],
            pltpu.SemaphoreType.DMA((steps, 2)),
            pltpu.SemaphoreType.DMA((steps, 2)),
            pltpu.SemaphoreType.DMA((1, len(tables))),
        ],
        compiler_params=params(0, 52 * 2**20),
        cost_estimate=pl.CostEstimate(
            flops=24 * split * kept * rows * LANES * 512, bytes_accessed=8 * x.size, transcendentals=0
        ),
        name="channels",
    )(x, f, *tables)


def lags_kernel(place_ref, spec_ref, mi_hbm, wi_hbm, tc_hbm, ts_hbm, *refs):
    *out_refs, spec, out_buf, mi_ref, wi_ref, tc_ref, ts_ref, in_sems, out_sems = refs
    ring, halves, kept, cuts, _ = out_buf.shape
    rows = spec.shape[1]
    moves = copies(
        [(spec_ref, spec), (mi_hbm, mi_ref), (tc_hbm, tc_ref), (ts_hbm, ts_ref), (wi_hbm, wi_ref)], in_sems, 0
    )
    start(moves)
    wait(moves)
    out = back(spec[...].reshape(kept * rows, 2 * LANES), mi_ref, wi_ref, tc_ref[...], ts_ref[...], kept, rows)
    out = out.astype(bf16)
    for place in range(ring * halves):
        at = place * cuts
        z, half = order(place, ring * halves)
        to = ((z - place_ref[0]) & (ring - 1), half ^ place_ref[1])
        for i in range(kept):
            out_buf[*to, i] = out[at : at + cuts, i * LANES : (i + 1) * LANES]
    moves = copies([(out_buf.at[z], out_refs[z]) for z in range(ring)], out_sems, 0)
    start(moves)
    wait(moves)


def lags(place, spec, t, n_tp, cuts):
    kept, rows, _ = spec.shape
    tables = [t[k] for k in (*CROSS_BACK, "turn_cos", "turn_sin")]
    ring = n_tp // SPLIT
    out = (SPLIT, kept, cuts, LANES)
    return pl.pallas_call(
        lags_kernel,
        in_specs=[pl.BlockSpec(memory_space=pltpu.SMEM)] + [ANY] * (1 + len(tables)),
        out_specs=[ANY] * ring,
        out_shape=[jax.ShapeDtypeStruct(out, bf16)] * ring,
        scratch_shapes=[
            pltpu.VMEM(spec.shape, bf16),
            pltpu.VMEM((ring, *out), bf16),
            *[pltpu.VMEM(v.shape, v.dtype) for v in tables],
            pltpu.SemaphoreType.DMA((1, 1 + len(tables))),
            pltpu.SemaphoreType.DMA((1, ring)),
        ],
        compiler_params=params(0),
        cost_estimate=pl.CostEstimate(
            flops=12 * kept * rows * LANES * 512, bytes_accessed=4 * spec.size, transcendentals=0
        ),
        name="lags",
    )(place, spec, *tables)


def order(place, n):
    return place % (n // SPLIT), place // (n // SPLIT)


def sum_scattered(parts, n):
    ring = n // SPLIT
    total = parts[0].astype(f32)
    for step in sorted(range(1, ring), key=lambda step: -min(step, ring - step)):
        pairs = [(i, i // ring * ring + (i + step) % ring) for i in range(n)]
        total = total + lax.ppermute(parts[step], "tp", pairs).astype(f32)
    return total


def body(query, key_in, value, grad_out, filter_raw, *, n_ctx, n_tp):
    group, length = filter_raw.shape
    rows = length // LANES
    kept = group // SPLIT
    root = 1.0 / math.sqrt(length)
    t = {k: jnp.asarray(v) for k, v in make_tables(length).items()}
    ring = n_tp // SPLIT
    sharing = [[c * n_tp + half * ring + z for c in range(n_ctx) for half in range(SPLIT)] for z in range(ring)]

    def exchange(x):
        flat = x.reshape(n_ctx * SPLIT, *x.shape[2:])
        flat = lax.all_to_all(
            flat, ("ctx", "tp"), split_axis=0, concat_axis=0, tiled=True, axis_index_groups=sharing
        )
        return flat.reshape(x.shape)

    place = order(lax.axis_index("tp"), n_tp)
    half = place[1]
    got = exchange(gate(query, key_in, value, grad_out, n_ctx))
    where = jnp.stack(place).astype(jnp.int32)
    filters = lax.dynamic_slice_in_dim(filter_raw, half * kept, kept, 0)
    filt = filter_spectrum(filters.reshape(kept, rows, LANES), t, root / length)
    filt, where = lax.optimization_barrier((filt, where))
    cross, made = channels(got, filt, t, root / length)
    tok = exchange(made)
    parts = lags(where, cross, t, n_tp, rows // n_ctx)
    total = sum_scattered(parts, n_tp)
    total = total.reshape(SPLIT, kept, length // n_tp)
    far = lax.ppermute(total[1], "tp", [(i, (i + ring) % n_tp) for i in range(n_tp)])
    grad_query, grad_key, grad_value = finish(tok, key_in, value, grad_out)
    mine, grad_query = lax.optimization_barrier((total[0], grad_query))
    filter_grad = jnp.where(jnp.arange(SPLIT)[:, None, None] == half, mine, far).reshape(group, length // n_tp)
    return (grad_query, grad_key, grad_value, filter_grad)


def solution(mesh):
    placed = (P("tp", "ctx"), P("tp", "ctx"), P("tp", "ctx"), P("tp", "ctx"), P("ctx", None))
    return jax.shard_map(
        functools.partial(body, n_ctx=mesh.shape["ctx"], n_tp=mesh.shape["tp"]),
        mesh=mesh,
        in_specs=placed,
        out_specs=(P("tp", "ctx"), P("tp", "ctx"), P("tp", "ctx"), P("ctx", "tp")),
        check_vma=False,
    )
```

```python
import functools
import math

import jax
import jax.numpy as jnp
import ml_dtypes
import numpy as np
from jax import lax
from jax.experimental import pallas as pl
from jax.experimental.pallas import tpu as pltpu
from jax.sharding import PartitionSpec as P

LANES = 128
VMEM_LIMIT = 56 * 2**20
SPLIT = 2
GATE_STEPS = 2
TOKEN_STEPS = 4
FILTERS = 4
FILTER_PAIR = 4
CROSS_BACK = ("mi", "wi")
TOKEN_BACK = ("mi", "wi")
f32 = jnp.float32
bf16 = jnp.bfloat16


def split_parts(table):
    high = table.astype(np.float32).astype(ml_dtypes.bfloat16)
    low = (table - high.astype(np.float64)).astype(np.float32).astype(ml_dtypes.bfloat16)
    return high, low


@functools.lru_cache(maxsize=None)
def make_tables(length):
    rows = length // LANES
    total = 2 * length
    a = np.arange(rows, dtype=np.float64)
    k1 = np.arange(rows, dtype=np.float64) + 0.5
    b = np.arange(LANES, dtype=np.float64)
    first = 2.0 * np.pi * np.outer(k1, a) / (2 * rows)
    turn = 2.0 * np.pi * np.outer(k1, b) / total
    second = 2.0 * np.pi * np.outer(b, b) / LANES
    c2, s2 = np.cos(second), np.sin(second)
    w_high, w_low = split_parts(np.concatenate([np.cos(first), -np.sin(first)], 0))
    m_high, m_low = split_parts(np.block([[c2, -s2], [s2, c2]]))
    mi_high, mi_low = split_parts(np.block([[c2, s2], [-s2, c2]]))
    wi_high, wi_low = split_parts(np.concatenate([np.cos(first).T, -np.sin(first).T], 1))
    return dict(
        w3=np.concatenate([w_high, w_low, w_high], 1),
        m3=np.concatenate([m_high, m_low, m_high], 0),
        w=w_high,
        m=m_high,
        mi=mi_high,
        wi=wi_high,
        mi2=np.concatenate([mi_high, mi_low], 0),
        wi2=np.concatenate([wi_high, wi_low], 1),
        turn_cos=np.cos(turn).astype(np.float32),
        turn_sin=np.sin(turn).astype(np.float32),
    )


def dot(x, y):
    return jnp.dot(x, y, preferred_element_type=f32)


def whole(table):
    return pl.BlockSpec(table.shape, lambda *_: (0,) * table.ndim)


def params(grid_rank, limit=VMEM_LIMIT):
    return pltpu.CompilerParams(
        dimension_semantics=("arbitrary",) * grid_rank if grid_rank else None,
        vmem_limit_bytes=limit,
    )


def swap_table(size):
    index = np.arange(size * size).reshape(size, size)
    table = np.zeros((size * size, size * size), np.float32)
    table[index.T.reshape(-1), index.reshape(-1)] = 1.0
    return table.astype(ml_dtypes.bfloat16)


def copies(pairs, sems, at):
    return [pltpu.make_async_copy(src, dst, sems.at[at, i]) for i, (src, dst) in enumerate(pairs)]


def start(moves):
    for move in moves:
        move.start()


def wait(moves):
    for move in moves:
        move.wait()


ANY = pl.BlockSpec(memory_space=pl.ANY)
VMEM = pl.BlockSpec(memory_space=pltpu.VMEM)


def gate_kernel(
    q_ref, k_ref, v_ref, g_ref, swap_hbm, out_ref, q, k, v, g, o, swap_ref, in_sems, out_sems, swap_sems
):
    n, split, _, kept, cuts, _ = out_ref.shape
    group = split * kept
    runs = n // GATE_STEPS

    def loads(step):
        rows = pl.ds(step * runs * group, runs * group)
        pairs = [(r.at[rows], s.at[rows]) for r, s in ((k_ref, k), (v_ref, v), (g_ref, g), (q_ref, q))]
        return copies(pairs, in_sems, step)

    def stores(step):
        at = pl.ds(step * runs, runs)
        return copies([(o.at[at], out_ref.at[at])], out_sems, step)

    swap = copies([(swap_hbm, swap_ref)], swap_sems, 0)
    start(swap)
    for step in range(GATE_STEPS):
        start(loads(step))
    wait(swap)
    for step in range(GATE_STEPS):
        wait(loads(step))
        for run in range(step * runs, (step + 1) * runs):
            rows = slice(run * group, (run + 1) * group)

            def product(x, y):
                z = x[rows, :] * y[rows, :]
                return jnp.concatenate([z[:, j * LANES : (j + 1) * LANES] for j in range(cuts)], 0)

            both = jnp.concatenate([product(k, v), product(g, q)], 1)
            out = dot(swap_ref[...], both).astype(bf16)
            for s in range(2):
                o[run, :, s] = out[:, s * LANES : (s + 1) * LANES].reshape(split, kept, cuts, LANES)
        start(stores(step))
    for step in range(GATE_STEPS):
        wait(stores(step))


def gate(query, key_in, value, grad_out, n):
    channels, length = query.shape
    group = channels // n
    cuts = length // LANES
    swap = jnp.asarray(swap_table(group))
    sent = (n, SPLIT, 2, group // SPLIT, cuts, LANES)
    return pl.pallas_call(
        gate_kernel,
        in_specs=[ANY] * 5,
        out_specs=ANY,
        out_shape=jax.ShapeDtypeStruct(sent, bf16),
        scratch_shapes=[pltpu.VMEM(query.shape, bf16)] * 4
        + [
            pltpu.VMEM(sent, bf16),
            pltpu.VMEM(swap.shape, bf16),
            pltpu.SemaphoreType.DMA((GATE_STEPS, 4)),
            pltpu.SemaphoreType.DMA((GATE_STEPS, 1)),
            pltpu.SemaphoreType.DMA((1, 1)),
        ],
        compiler_params=params(0),
        cost_estimate=pl.CostEstimate(
            flops=2 * channels * length, bytes_accessed=12 * channels * length, transcendentals=0
        ),
        name="gate",
    )(query, key_in, value, grad_out, swap)


def finish_kernel(
    tok_ref, k_ref, v_ref, g_ref, swap_ref, gq_ref, gk_ref, gv_ref, tok, k, v, g, gq, gk, gv, in_sems, out_sems
):
    n, split, _, kept, cuts, _ = tok_ref.shape
    group = split * kept
    runs = n // TOKEN_STEPS

    def loads(step):
        rows = pl.ds(step * runs * group, runs * group)
        at = pl.ds(step * runs, runs)
        pairs = [(tok_ref.at[at], tok.at[at])]
        pairs += [(r.at[rows], s.at[rows]) for r, s in ((g_ref, g), (v_ref, v), (k_ref, k))]
        return copies(pairs, in_sems, step)

    def stores(step):
        rows = pl.ds(step * runs * group, runs * group)
        pairs = [(s.at[rows], r.at[rows]) for r, s in ((gq_ref, gq), (gk_ref, gk), (gv_ref, gv))]
        return copies(pairs, out_sems, step)

    for step in range(TOKEN_STEPS):
        start(loads(step))
    for step in range(TOKEN_STEPS):
        wait(loads(step))
        for run in range(step * runs, (step + 1) * runs):
            rows = slice(run * group, (run + 1) * group)
            both = jnp.concatenate([tok[run, :, s].reshape(group * cuts, LANES) for s in range(2)], 1)
            out = dot(swap_ref[...], both).astype(bf16)
            for j in range(cuts):
                lanes = slice(j * LANES, (j + 1) * LANES)
                conv = out[j * group : (j + 1) * group, :LANES]
                dgated = out[j * group : (j + 1) * group, LANES:]
                gq[rows, lanes] = g[rows, lanes] * conv
                gk[rows, lanes] = dgated * v[rows, lanes]
                gv[rows, lanes] = dgated * k[rows, lanes]
        start(stores(step))
    for step in range(TOKEN_STEPS):
        wait(stores(step))


def finish(tok, key_in, value, grad_out):
    group = tok.shape[1] * tok.shape[3]
    channels, length = key_in.shape
    swap = jnp.asarray(swap_table(group))
    return pl.pallas_call(
        finish_kernel,
        in_specs=[ANY] * 4 + [VMEM],
        out_specs=[ANY] * 3,
        out_shape=[jax.ShapeDtypeStruct((channels, length), bf16)] * 3,
        scratch_shapes=[pltpu.VMEM(tok.shape, bf16)]
        + [pltpu.VMEM(key_in.shape, bf16)] * 6
        + [pltpu.SemaphoreType.DMA((TOKEN_STEPS, 4)), pltpu.SemaphoreType.DMA((TOKEN_STEPS, 3))],
        compiler_params=params(0, 52 * 2**20),
        cost_estimate=pl.CostEstimate(
            flops=3 * channels * length, bytes_accessed=16 * channels * length, transcendentals=0
        ),
        name="finish",
    )(tok, key_in, value, grad_out, swap)


def turned(stage, turn_cos, turn_sin, rows, at):
    lanes = slice(at * LANES, (at + 1) * LANES)
    re, im = stage[:rows, lanes], stage[rows:, lanes]
    return jnp.concatenate([re * turn_cos + im * turn_sin, im * turn_cos - re * turn_sin], 1)


def filter_kernel(x_ref, w_ref, m_ref, tc_ref, ts_ref, out_ref, *, scale):
    pair, rows, _ = x_ref.shape
    x = jnp.concatenate([x_ref[i] for i in range(pair)], 1)
    high = x.astype(bf16)
    low = (x - high.astype(f32)).astype(bf16)
    stage = dot(w_ref[...], jnp.concatenate([high, high, low], 0))
    for i in range(pair):
        u = turned(stage, tc_ref[...], ts_ref[...], rows, i) * scale
        u_high = u.astype(bf16)
        u_low = (u - u_high.astype(f32)).astype(bf16)
        out_ref[i] = dot(jnp.concatenate([u_high, u_high, u_low], 1), m_ref[...])


def filter_spectrum(filt, t, scale):
    n, rows, _ = filt.shape
    pair = FILTER_PAIR
    tables = [t["w3"], t["m3"], t["turn_cos"], t["turn_sin"]]
    return pl.pallas_call(
        functools.partial(filter_kernel, scale=scale),
        grid=(n // pair,),
        in_specs=[pl.BlockSpec((pair, rows, LANES), lambda i: (i, 0, 0))] + [whole(x) for x in tables],
        out_specs=pl.BlockSpec((pair, rows, 2 * LANES), lambda i: (i, 0, 0)),
        out_shape=jax.ShapeDtypeStruct((n, rows, 2 * LANES), f32),
        compiler_params=params(1),
        cost_estimate=pl.CostEstimate(
            flops=12 * n * rows * LANES * 512, bytes_accessed=16 * n * rows * LANES, transcendentals=0
        ),
        name="filter_spectrum",
    )(filt, *tables)


def back(spec, mi_ref, wi_ref, bc, bs, pair, rows):
    parts = mi_ref.shape[0] // (2 * LANES)
    stage = dot(jnp.concatenate([spec] * parts, 1), mi_ref[...])
    re_parts, im_parts = [], []
    for i in range(pair):
        re = stage[i * rows : (i + 1) * rows, :LANES]
        im = stage[i * rows : (i + 1) * rows, LANES:]
        re_parts.append((re * bc - im * bs).astype(bf16))
        im_parts.append((re * bs + im * bc).astype(bf16))
    v = jnp.concatenate([jnp.concatenate(re_parts, 1), jnp.concatenate(im_parts, 1)], 0)
    return dot(wi_ref[...], jnp.concatenate([v] * parts, 0))


def channels_kernel(
    x_ref, f_ref, w_hbm, m_hbm, tc_hbm, ts_hbm, mi_hbm, wi_hbm, cross_ref, out_ref,
    x_buf, f_buf, cross_buf, out_buf, w_ref, m_ref, tc_ref, ts_ref, mi_ref, wi_ref,
    in_sems, out_sems, table_sems,
):
    n, split, _, kept, cuts, _ = x_ref.shape
    steps, count = f_buf.shape[:2]
    rows = n * cuts

    def loads(step):
        at = pl.ds(step * count, count)
        return copies([(x_ref.at[:, :, :, at], x_buf.at[step]), (f_ref.at[at], f_buf.at[step])], in_sems, step)

    def stores(step):
        at = pl.ds(step * count, count)
        return copies(
            [(cross_buf.at[step], cross_ref.at[at]), (out_buf.at[step], out_ref.at[:, :, :, at])], out_sems, step
        )

    tables = copies(
        [(w_hbm, w_ref), (tc_hbm, tc_ref), (ts_hbm, ts_ref), (m_hbm, m_ref), (mi_hbm, mi_ref), (wi_hbm, wi_ref)],
        table_sems, 0,
    )
    start(loads(0))
    start(tables)
    for step in range(1, steps):
        start(loads(step))
    wait(tables)

    @pl.loop(0, steps)
    def _(step):
        wait(loads(step))
        places = [(m, i) for i in range(count) for m in range(split)]
        us = []
        for m, i in places:
            x = jnp.concatenate([x_buf[step, :, m, s, i].reshape(rows, LANES) for s in range(2)], 1)
            stage = dot(w_ref[...], x)
            us += [turned(stage, tc_ref[...], ts_ref[...], rows, s).astype(bf16) for s in range(2)]
        spec = dot(jnp.concatenate(us, 0), m_ref[...])
        parts, cross = [], []
        for at, (m, i) in enumerate(places):
            fr, fi = f_buf[step, i, :, :LANES], f_buf[step, i, :, LANES:]
            g, d = (spec[(2 * at + s) * rows : (2 * at + s + 1) * rows] for s in range(2))
            gr, gi, dr, di = g[:, :LANES], g[:, LANES:], d[:, :LANES], d[:, LANES:]
            cross.append((dr * gr + di * gi, di * gr - dr * gi))
            parts.append(jnp.concatenate([fr * gr - fi * gi, fr * gi + fi * gr], 1).astype(bf16))
            parts.append(jnp.concatenate([dr * fr + di * fi, di * fr - dr * fi], 1).astype(bf16))
        for i in range(count):
            terms = zip(*cross[i * split : (i + 1) * split])
            cross_buf[step, i] = jnp.concatenate([sum(part) for part in terms], 1).astype(bf16)
        made = back(jnp.concatenate(parts, 0), mi_ref, wi_ref, tc_ref[...], ts_ref[...], len(parts), rows)
        made = made.astype(bf16)
        for at, (m, i) in enumerate(places):
            for s in range(2):
                lanes = slice((2 * at + s) * LANES, (2 * at + s + 1) * LANES)
                out_buf[step, :, m, s, i] = made[:, lanes].reshape(n, cuts, LANES)
        start(stores(step))

    for step in range(steps):
        wait(stores(step))


def channels(x, f, t):
    n, split, _, kept, cuts, _ = x.shape
    rows = n * cuts
    count = FILTERS
    steps = kept // count
    tables = [t[k] for k in ("w", "m", "turn_cos", "turn_sin", *TOKEN_BACK)]
    spec = (count, rows, 2 * LANES)
    block = (steps, n, split, 2, count, cuts, LANES)
    return pl.pallas_call(
        channels_kernel,
        in_specs=[ANY] * (2 + len(tables)),
        out_specs=[ANY] * 2,
        out_shape=[jax.ShapeDtypeStruct((kept, rows, 2 * LANES), bf16), jax.ShapeDtypeStruct(x.shape, bf16)],
        scratch_shapes=[
            pltpu.VMEM(block, bf16),
            pltpu.VMEM((steps, *spec), f32),
            pltpu.VMEM((steps, *spec), bf16),
            pltpu.VMEM(block, bf16),
            *[pltpu.VMEM(v.shape, v.dtype) for v in tables],
            pltpu.SemaphoreType.DMA((steps, 2)),
            pltpu.SemaphoreType.DMA((steps, 2)),
            pltpu.SemaphoreType.DMA((1, len(tables))),
        ],
        compiler_params=params(0, 52 * 2**20),
        cost_estimate=pl.CostEstimate(
            flops=24 * split * kept * rows * LANES * 512, bytes_accessed=8 * x.size, transcendentals=0
        ),
        name="channels",
    )(x, f, *tables)


def lags_kernel(place_ref, spec_ref, mi_hbm, wi_hbm, tc_hbm, ts_hbm, *refs, scale):
    *out_refs, spec, out_buf, mi_ref, wi_ref, tc_ref, ts_ref, in_sems, out_sems = refs
    ring, halves, kept, cuts, _ = out_buf.shape
    rows = spec.shape[1]
    moves = copies(
        [(spec_ref, spec), (mi_hbm, mi_ref), (tc_hbm, tc_ref), (ts_hbm, ts_ref), (wi_hbm, wi_ref)], in_sems, 0
    )
    start(moves)
    wait(moves)
    out = back(spec[...].reshape(kept * rows, 2 * LANES), mi_ref, wi_ref, tc_ref[...], ts_ref[...], kept, rows)
    out = (out * scale).astype(bf16)
    for place in range(ring * halves):
        at = place * cuts
        z, half = order(place, ring * halves)
        to = ((z - place_ref[0]) & (ring - 1), half ^ place_ref[1])
        for i in range(kept):
            out_buf[*to, i] = out[at : at + cuts, i * LANES : (i + 1) * LANES]
    moves = copies([(out_buf.at[z], out_refs[z]) for z in range(ring)], out_sems, 0)
    start(moves)
    wait(moves)


def lags(place, spec, t, scale, n_tp, cuts):
    kept, rows, _ = spec.shape
    tables = [t[k] for k in (*CROSS_BACK, "turn_cos", "turn_sin")]
    ring = n_tp // SPLIT
    out = (SPLIT, kept, cuts, LANES)
    return pl.pallas_call(
        functools.partial(lags_kernel, scale=scale),
        in_specs=[pl.BlockSpec(memory_space=pltpu.SMEM)] + [ANY] * (1 + len(tables)),
        out_specs=[ANY] * ring,
        out_shape=[jax.ShapeDtypeStruct(out, bf16)] * ring,
        scratch_shapes=[
            pltpu.VMEM(spec.shape, bf16),
            pltpu.VMEM((ring, *out), bf16),
            *[pltpu.VMEM(v.shape, v.dtype) for v in tables],
            pltpu.SemaphoreType.DMA((1, 1 + len(tables))),
            pltpu.SemaphoreType.DMA((1, ring)),
        ],
        compiler_params=params(0),
        cost_estimate=pl.CostEstimate(
            flops=12 * kept * rows * LANES * 512, bytes_accessed=4 * spec.size, transcendentals=0
        ),
        name="lags",
    )(place, spec, *tables)


def order(place, n):
    return place % (n // SPLIT), place // (n // SPLIT)


def sum_scattered(parts, n):
    ring = n // SPLIT
    total = parts[0].astype(f32)
    for step in sorted(range(1, ring), key=lambda step: -min(step, ring - step)):
        pairs = [(i, i // ring * ring + (i + step) % ring) for i in range(n)]
        total = total + lax.ppermute(parts[step], "tp", pairs).astype(f32)
    return total


def body(query, key_in, value, grad_out, filter_raw, *, n_ctx, n_tp):
    group, length = filter_raw.shape
    rows = length // LANES
    kept = group // SPLIT
    root = 1.0 / math.sqrt(length)
    t = {k: jnp.asarray(v) for k, v in make_tables(length).items()}
    ring = n_tp // SPLIT
    sharing = [[c * n_tp + half * ring + z for c in range(n_ctx) for half in range(SPLIT)] for z in range(ring)]

    def exchange(x):
        flat = x.reshape(n_ctx * SPLIT, *x.shape[2:])
        flat = lax.all_to_all(
            flat, ("ctx", "tp"), split_axis=0, concat_axis=0, tiled=True, axis_index_groups=sharing
        )
        return flat.reshape(x.shape)

    place = order(lax.axis_index("tp"), n_tp)
    half = place[1]
    got = exchange(gate(query, key_in, value, grad_out, n_ctx))
    where = jnp.stack(place).astype(jnp.int32)
    filters = lax.dynamic_slice_in_dim(filter_raw, half * kept, kept, 0)
    filt = filter_spectrum(filters.reshape(kept, rows, LANES), t, root / length)
    filt, where = lax.optimization_barrier((filt, where))
    cross, made = channels(got, filt, t)
    tok = exchange(made)
    parts = lags(where, cross, t, root / length, n_tp, rows // n_ctx)
    total = sum_scattered(parts, n_tp)
    total = total.reshape(SPLIT, kept, length // n_tp)
    far = lax.ppermute(total[1], "tp", [(i, (i + ring) % n_tp) for i in range(n_tp)])
    grad_query, grad_key, grad_value = finish(tok, key_in, value, grad_out)
    mine, grad_query = lax.optimization_barrier((total[0], grad_query))
    filter_grad = jnp.where(jnp.arange(SPLIT)[:, None, None] == half, mine, far).reshape(group, length // n_tp)
    return (grad_query, grad_key, grad_value, filter_grad)


def solution(mesh):
    placed = (P("tp", "ctx"), P("tp", "ctx"), P("tp", "ctx"), P("tp", "ctx"), P("ctx", None))
    return jax.shard_map(
        functools.partial(body, n_ctx=mesh.shape["ctx"], n_tp=mesh.shape["tp"]),
        mesh=mesh,
        in_specs=placed,
        out_specs=(P("tp", "ctx"), P("tp", "ctx"), P("tp", "ctx"), P("ctx", "tp")),
        check_vma=False,
    )
```

```python
import functools
import math

import jax
import jax.numpy as jnp
import ml_dtypes
import numpy as np
from jax import lax
from jax.experimental import pallas as pl
from jax.experimental.pallas import tpu as pltpu
from jax.sharding import PartitionSpec as P

LANES = 128
VMEM_LIMIT = 56 * 2**20
SPLIT = 2
GATE_STEPS = 2
FINISH_ENDS = (4, 9, 13, 16)
FILTERS = 4
FILTER_PAIR = 4
CROSS_BACK = ("mi", "wi")
TOKEN_BACK = ("mi", "wi")
f32 = jnp.float32
bf16 = jnp.bfloat16


def split_parts(table):
    high = table.astype(np.float32).astype(ml_dtypes.bfloat16)
    low = (table - high.astype(np.float64)).astype(np.float32).astype(ml_dtypes.bfloat16)
    return high, low


@functools.lru_cache(maxsize=None)
def make_tables(length):
    rows = length // LANES
    total = 2 * length
    a = np.arange(rows, dtype=np.float64)
    k1 = np.arange(rows, dtype=np.float64) + 0.5
    b = np.arange(LANES, dtype=np.float64)
    first = 2.0 * np.pi * np.outer(k1, a) / (2 * rows)
    turn = 2.0 * np.pi * np.outer(k1, b) / total
    second = 2.0 * np.pi * np.outer(b, b) / LANES
    c2, s2 = np.cos(second), np.sin(second)
    w_high, w_low = split_parts(np.concatenate([np.cos(first), -np.sin(first)], 0))
    m_high, m_low = split_parts(np.block([[c2, -s2], [s2, c2]]))
    mi_high, mi_low = split_parts(np.block([[c2, s2], [-s2, c2]]))
    wi_high, wi_low = split_parts(np.concatenate([np.cos(first).T, -np.sin(first).T], 1))
    return dict(
        w3=np.concatenate([w_high, w_low, w_high], 1),
        m3=np.concatenate([m_high, m_low, m_high], 0),
        w=w_high,
        m=m_high,
        mi=mi_high,
        wi=wi_high,
        mi2=np.concatenate([mi_high, mi_low], 0),
        wi2=np.concatenate([wi_high, wi_low], 1),
        turn_cos=np.cos(turn).astype(np.float32),
        turn_sin=np.sin(turn).astype(np.float32),
    )


def dot(x, y):
    return jnp.dot(x, y, preferred_element_type=f32)


def whole(table):
    return pl.BlockSpec(table.shape, lambda *_: (0,) * table.ndim)


def params(grid_rank, limit=VMEM_LIMIT):
    return pltpu.CompilerParams(
        dimension_semantics=("arbitrary",) * grid_rank if grid_rank else None,
        vmem_limit_bytes=limit,
    )


def swap_table(size):
    index = np.arange(size * size).reshape(size, size)
    table = np.zeros((size * size, size * size), np.float32)
    table[index.T.reshape(-1), index.reshape(-1)] = 1.0
    return table.astype(ml_dtypes.bfloat16)


def copies(pairs, sems, at):
    return [pltpu.make_async_copy(src, dst, sems.at[at, i]) for i, (src, dst) in enumerate(pairs)]


def start(moves):
    for move in moves:
        move.start()


def wait(moves):
    for move in moves:
        move.wait()


ANY = pl.BlockSpec(memory_space=pl.ANY)
VMEM = pl.BlockSpec(memory_space=pltpu.VMEM)


def gate_kernel(
    q_ref, k_ref, v_ref, g_ref, swap_hbm, out_ref, q, k, v, g, o, swap_ref, in_sems, out_sems, swap_sems
):
    n, split, _, kept, cuts, _ = out_ref.shape
    group = split * kept
    runs = n // GATE_STEPS

    def loads(step):
        rows = pl.ds(step * runs * group, runs * group)
        pairs = [(r.at[rows], s.at[rows]) for r, s in ((k_ref, k), (v_ref, v), (g_ref, g), (q_ref, q))]
        return copies(pairs, in_sems, step)

    def stores(step):
        at = pl.ds(step * runs, runs)
        return copies([(o.at[at], out_ref.at[at])], out_sems, step)

    swap = copies([(swap_hbm, swap_ref)], swap_sems, 0)
    start(swap)
    for step in range(GATE_STEPS):
        start(loads(step))
    wait(swap)
    for step in range(GATE_STEPS):
        wait(loads(step))
        for run in range(step * runs, (step + 1) * runs):
            rows = slice(run * group, (run + 1) * group)

            def product(x, y):
                z = x[rows, :] * y[rows, :]
                return jnp.concatenate([z[:, j * LANES : (j + 1) * LANES] for j in range(cuts)], 0)

            both = jnp.concatenate([product(k, v), product(g, q)], 1)
            out = dot(swap_ref[...], both).astype(bf16)
            for s in range(2):
                o[run, :, s] = out[:, s * LANES : (s + 1) * LANES].reshape(split, kept, cuts, LANES)
        start(stores(step))
    for step in range(GATE_STEPS):
        wait(stores(step))


def gate(query, key_in, value, grad_out, n):
    channels, length = query.shape
    group = channels // n
    cuts = length // LANES
    swap = jnp.asarray(swap_table(group))
    sent = (n, SPLIT, 2, group // SPLIT, cuts, LANES)
    return pl.pallas_call(
        gate_kernel,
        in_specs=[ANY] * 5,
        out_specs=ANY,
        out_shape=jax.ShapeDtypeStruct(sent, bf16),
        scratch_shapes=[pltpu.VMEM(query.shape, bf16)] * 4
        + [
            pltpu.VMEM(sent, bf16),
            pltpu.VMEM(swap.shape, bf16),
            pltpu.SemaphoreType.DMA((GATE_STEPS, 4)),
            pltpu.SemaphoreType.DMA((GATE_STEPS, 1)),
            pltpu.SemaphoreType.DMA((1, 1)),
        ],
        compiler_params=params(0),
        cost_estimate=pl.CostEstimate(
            flops=2 * channels * length, bytes_accessed=12 * channels * length, transcendentals=0
        ),
        name="gate",
    )(query, key_in, value, grad_out, swap)


def finish_kernel(
    tok_ref, k_ref, v_ref, g_ref, swap_ref, gq_ref, gk_ref, gv_ref, tok, k, v, g, gq, gk, gv, in_sems, out_sems
):
    n, split, _, kept, cuts, _ = tok_ref.shape
    group = split * kept
    ends = [n * part // 16 for part in FINISH_ENDS]
    begins = [0, *ends[:-1]]

    def loads(step):
        rows = pl.ds(begins[step] * group, (ends[step] - begins[step]) * group)
        at = pl.ds(begins[step], ends[step] - begins[step])
        pairs = [(tok_ref.at[at], tok.at[at])]
        pairs += [(r.at[rows], s.at[rows]) for r, s in ((g_ref, g), (v_ref, v), (k_ref, k))]
        return copies(pairs, in_sems, step)

    def stores(step):
        rows = pl.ds(begins[step] * group, (ends[step] - begins[step]) * group)
        pairs = [(s.at[rows], r.at[rows]) for r, s in ((gq_ref, gq), (gk_ref, gk), (gv_ref, gv))]
        return copies(pairs, out_sems, step)

    for step in range(len(FINISH_ENDS)):
        start(loads(step))
    for step in range(len(FINISH_ENDS)):
        wait(loads(step))
        for run in range(begins[step], ends[step]):
            rows = slice(run * group, (run + 1) * group)
            both = jnp.concatenate([tok[run, :, s].reshape(group * cuts, LANES) for s in range(2)], 1)
            out = dot(swap_ref[...], both).astype(bf16)
            for j in range(cuts):
                lanes = slice(j * LANES, (j + 1) * LANES)
                conv = out[j * group : (j + 1) * group, :LANES]
                dgated = out[j * group : (j + 1) * group, LANES:]
                gq[rows, lanes] = g[rows, lanes] * conv
                gk[rows, lanes] = dgated * v[rows, lanes]
                gv[rows, lanes] = dgated * k[rows, lanes]
        start(stores(step))
    for step in range(len(FINISH_ENDS)):
        wait(stores(step))


def finish(tok, key_in, value, grad_out):
    group = tok.shape[1] * tok.shape[3]
    channels, length = key_in.shape
    swap = jnp.asarray(swap_table(group))
    return pl.pallas_call(
        finish_kernel,
        in_specs=[ANY] * 4 + [VMEM],
        out_specs=[ANY] * 3,
        out_shape=[jax.ShapeDtypeStruct((channels, length), bf16)] * 3,
        scratch_shapes=[pltpu.VMEM(tok.shape, bf16)]
        + [pltpu.VMEM(key_in.shape, bf16)] * 6
        + [pltpu.SemaphoreType.DMA((len(FINISH_ENDS), 4)), pltpu.SemaphoreType.DMA((len(FINISH_ENDS), 3))],
        compiler_params=params(0, 52 * 2**20),
        cost_estimate=pl.CostEstimate(
            flops=3 * channels * length, bytes_accessed=16 * channels * length, transcendentals=0
        ),
        name="finish",
    )(tok, key_in, value, grad_out, swap)


def turned(stage, turn_cos, turn_sin, rows, at):
    lanes = slice(at * LANES, (at + 1) * LANES)
    re, im = stage[:rows, lanes], stage[rows:, lanes]
    return jnp.concatenate([re * turn_cos + im * turn_sin, im * turn_cos - re * turn_sin], 1)


def filter_kernel(x_ref, w_ref, m_ref, tc_ref, ts_ref, out_ref, *, scale):
    pair, rows, _ = x_ref.shape
    x = jnp.concatenate([x_ref[i] for i in range(pair)], 1)
    high = x.astype(bf16)
    low = (x - high.astype(f32)).astype(bf16)
    stage = dot(w_ref[...], jnp.concatenate([high, high, low], 0))
    for i in range(pair):
        u = turned(stage, tc_ref[...], ts_ref[...], rows, i) * scale
        u_high = u.astype(bf16)
        u_low = (u - u_high.astype(f32)).astype(bf16)
        out_ref[i] = dot(jnp.concatenate([u_high, u_high, u_low], 1), m_ref[...])


def filter_spectrum(filt, t, scale):
    n, rows, _ = filt.shape
    pair = FILTER_PAIR
    tables = [t["w3"], t["m3"], t["turn_cos"], t["turn_sin"]]
    return pl.pallas_call(
        functools.partial(filter_kernel, scale=scale),
        grid=(n // pair,),
        in_specs=[pl.BlockSpec((pair, rows, LANES), lambda i: (i, 0, 0))] + [whole(x) for x in tables],
        out_specs=pl.BlockSpec((pair, rows, 2 * LANES), lambda i: (i, 0, 0)),
        out_shape=jax.ShapeDtypeStruct((n, rows, 2 * LANES), f32),
        compiler_params=params(1),
        cost_estimate=pl.CostEstimate(
            flops=12 * n * rows * LANES * 512, bytes_accessed=16 * n * rows * LANES, transcendentals=0
        ),
        name="filter_spectrum",
    )(filt, *tables)


def back(spec, mi_ref, wi_ref, bc, bs, pair, rows):
    parts = mi_ref.shape[0] // (2 * LANES)
    stage = dot(jnp.concatenate([spec] * parts, 1), mi_ref[...])
    re_parts, im_parts = [], []
    for i in range(pair):
        re = stage[i * rows : (i + 1) * rows, :LANES]
        im = stage[i * rows : (i + 1) * rows, LANES:]
        re_parts.append((re * bc - im * bs).astype(bf16))
        im_parts.append((re * bs + im * bc).astype(bf16))
    v = jnp.concatenate([jnp.concatenate(re_parts, 1), jnp.concatenate(im_parts, 1)], 0)
    return dot(wi_ref[...], jnp.concatenate([v] * parts, 0))


def channels_kernel(
    x_ref, f_ref, w_hbm, m_hbm, tc_hbm, ts_hbm, mi_hbm, wi_hbm, cross_ref, out_ref,
    x_buf, f_buf, cross_buf, out_buf, w_ref, m_ref, tc_ref, ts_ref, mi_ref, wi_ref,
    in_sems, out_sems, table_sems,
):
    n, split, _, kept, cuts, _ = x_ref.shape
    steps, count = f_buf.shape[:2]
    rows = n * cuts

    def loads(step):
        at = pl.ds(step * count, count)
        return copies([(x_ref.at[:, :, :, at], x_buf.at[step]), (f_ref.at[at], f_buf.at[step])], in_sems, step)

    def stores(step):
        at = pl.ds(step * count, count)
        return copies(
            [(cross_buf.at[step], cross_ref.at[at]), (out_buf.at[step], out_ref.at[:, :, :, at])], out_sems, step
        )

    tables = copies(
        [(w_hbm, w_ref), (tc_hbm, tc_ref), (ts_hbm, ts_ref), (m_hbm, m_ref), (mi_hbm, mi_ref), (wi_hbm, wi_ref)],
        table_sems, 0,
    )
    start(loads(0))
    start(tables)
    for step in range(1, steps):
        start(loads(step))
    wait(tables)

    @pl.loop(0, steps)
    def _(step):
        wait(loads(step))
        places = [(m, i) for i in range(count) for m in range(split)]
        us = []
        for m, i in places:
            x = jnp.concatenate([x_buf[step, :, m, s, i].reshape(rows, LANES) for s in range(2)], 1)
            stage = dot(w_ref[...], x)
            us += [turned(stage, tc_ref[...], ts_ref[...], rows, s).astype(bf16) for s in range(2)]
        spec = dot(jnp.concatenate(us, 0), m_ref[...])
        parts, cross = [], []
        for at, (m, i) in enumerate(places):
            fr, fi = f_buf[step, i, :, :LANES], f_buf[step, i, :, LANES:]
            g, d = (spec[(2 * at + s) * rows : (2 * at + s + 1) * rows] for s in range(2))
            gr, gi, dr, di = g[:, :LANES], g[:, LANES:], d[:, :LANES], d[:, LANES:]
            cross.append((dr * gr + di * gi, di * gr - dr * gi))
            parts.append(jnp.concatenate([fr * gr - fi * gi, fr * gi + fi * gr], 1).astype(bf16))
            parts.append(jnp.concatenate([dr * fr + di * fi, di * fr - dr * fi], 1).astype(bf16))
        for i in range(count):
            terms = zip(*cross[i * split : (i + 1) * split])
            cross_buf[step, i] = jnp.concatenate([sum(part) for part in terms], 1).astype(bf16)
        made = back(jnp.concatenate(parts, 0), mi_ref, wi_ref, tc_ref[...], ts_ref[...], len(parts), rows)
        made = made.astype(bf16)
        for at, (m, i) in enumerate(places):
            for s in range(2):
                lanes = slice((2 * at + s) * LANES, (2 * at + s + 1) * LANES)
                out_buf[step, :, m, s, i] = made[:, lanes].reshape(n, cuts, LANES)
        start(stores(step))

    for step in range(steps):
        wait(stores(step))


def channels(x, f, t):
    n, split, _, kept, cuts, _ = x.shape
    rows = n * cuts
    count = FILTERS
    steps = kept // count
    tables = [t[k] for k in ("w", "m", "turn_cos", "turn_sin", *TOKEN_BACK)]
    spec = (count, rows, 2 * LANES)
    block = (steps, n, split, 2, count, cuts, LANES)
    return pl.pallas_call(
        channels_kernel,
        in_specs=[ANY] * (2 + len(tables)),
        out_specs=[ANY] * 2,
        out_shape=[jax.ShapeDtypeStruct((kept, rows, 2 * LANES), bf16), jax.ShapeDtypeStruct(x.shape, bf16)],
        scratch_shapes=[
            pltpu.VMEM(block, bf16),
            pltpu.VMEM((steps, *spec), f32),
            pltpu.VMEM((steps, *spec), bf16),
            pltpu.VMEM(block, bf16),
            *[pltpu.VMEM(v.shape, v.dtype) for v in tables],
            pltpu.SemaphoreType.DMA((steps, 2)),
            pltpu.SemaphoreType.DMA((steps, 2)),
            pltpu.SemaphoreType.DMA((1, len(tables))),
        ],
        compiler_params=params(0, 52 * 2**20),
        cost_estimate=pl.CostEstimate(
            flops=24 * split * kept * rows * LANES * 512, bytes_accessed=8 * x.size, transcendentals=0
        ),
        name="channels",
    )(x, f, *tables)


def lags_kernel(place_ref, spec_ref, mi_hbm, wi_hbm, tc_hbm, ts_hbm, *refs, scale):
    *out_refs, spec, out_buf, mi_ref, wi_ref, tc_ref, ts_ref, in_sems, out_sems = refs
    ring, halves, kept, cuts, _ = out_buf.shape
    rows = spec.shape[1]
    moves = copies(
        [(spec_ref, spec), (mi_hbm, mi_ref), (tc_hbm, tc_ref), (ts_hbm, ts_ref), (wi_hbm, wi_ref)], in_sems, 0
    )
    start(moves)
    wait(moves)
    out = back(spec[...].reshape(kept * rows, 2 * LANES), mi_ref, wi_ref, tc_ref[...], ts_ref[...], kept, rows)
    out = (out * scale).astype(bf16)
    for place in range(ring * halves):
        at = place * cuts
        z, half = order(place, ring * halves)
        to = ((z - place_ref[0]) & (ring - 1), half ^ place_ref[1])
        for i in range(kept):
            out_buf[*to, i] = out[at : at + cuts, i * LANES : (i + 1) * LANES]
    moves = copies([(out_buf.at[z], out_refs[z]) for z in range(ring)], out_sems, 0)
    start(moves)
    wait(moves)


def lags(place, spec, t, scale, n_tp, cuts):
    kept, rows, _ = spec.shape
    tables = [t[k] for k in (*CROSS_BACK, "turn_cos", "turn_sin")]
    ring = n_tp // SPLIT
    out = (SPLIT, kept, cuts, LANES)
    return pl.pallas_call(
        functools.partial(lags_kernel, scale=scale),
        in_specs=[pl.BlockSpec(memory_space=pltpu.SMEM)] + [ANY] * (1 + len(tables)),
        out_specs=[ANY] * ring,
        out_shape=[jax.ShapeDtypeStruct(out, bf16)] * ring,
        scratch_shapes=[
            pltpu.VMEM(spec.shape, bf16),
            pltpu.VMEM((ring, *out), bf16),
            *[pltpu.VMEM(v.shape, v.dtype) for v in tables],
            pltpu.SemaphoreType.DMA((1, 1 + len(tables))),
            pltpu.SemaphoreType.DMA((1, ring)),
        ],
        compiler_params=params(0),
        cost_estimate=pl.CostEstimate(
            flops=12 * kept * rows * LANES * 512, bytes_accessed=4 * spec.size, transcendentals=0
        ),
        name="lags",
    )(place, spec, *tables)


def order(place, n):
    return place % (n // SPLIT), place // (n // SPLIT)


def sum_scattered(parts, n):
    ring = n // SPLIT
    total = parts[0].astype(f32)
    for step in sorted(range(1, ring), key=lambda step: -min(step, ring - step)):
        pairs = [(i, i // ring * ring + (i + step) % ring) for i in range(n)]
        total = total + lax.ppermute(parts[step], "tp", pairs).astype(f32)
    return total


def body(query, key_in, value, grad_out, filter_raw, *, n_ctx, n_tp):
    group, length = filter_raw.shape
    rows = length // LANES
    kept = group // SPLIT
    root = 1.0 / math.sqrt(length)
    t = {k: jnp.asarray(v) for k, v in make_tables(length).items()}
    ring = n_tp // SPLIT
    sharing = [[c * n_tp + half * ring + z for c in range(n_ctx) for half in range(SPLIT)] for z in range(ring)]

    def exchange(x):
        flat = x.reshape(n_ctx * SPLIT, *x.shape[2:])
        flat = lax.all_to_all(
            flat, ("ctx", "tp"), split_axis=0, concat_axis=0, tiled=True, axis_index_groups=sharing
        )
        return flat.reshape(x.shape)

    place = order(lax.axis_index("tp"), n_tp)
    half = place[1]
    got = exchange(gate(query, key_in, value, grad_out, n_ctx))
    where = jnp.stack(place).astype(jnp.int32)
    filters = lax.dynamic_slice_in_dim(filter_raw, half * kept, kept, 0)
    filt = filter_spectrum(filters.reshape(kept, rows, LANES), t, root / length)
    filt, where = lax.optimization_barrier((filt, where))
    cross, made = channels(got, filt, t)
    tok = exchange(made)
    parts = lags(where, cross, t, root / length, n_tp, rows // n_ctx)
    total = sum_scattered(parts, n_tp)
    total = total.reshape(SPLIT, kept, length // n_tp)
    far = lax.ppermute(total[1], "tp", [(i, (i + ring) % n_tp) for i in range(n_tp)])
    grad_query, grad_key, grad_value = finish(tok, key_in, value, grad_out)
    mine, grad_query = lax.optimization_barrier((total[0], grad_query))
    filter_grad = jnp.where(jnp.arange(SPLIT)[:, None, None] == half, mine, far).reshape(group, length // n_tp)
    return (grad_query, grad_key, grad_value, filter_grad)


def solution(mesh):
    placed = (P("tp", "ctx"), P("tp", "ctx"), P("tp", "ctx"), P("tp", "ctx"), P("ctx", None))
    return jax.shard_map(
        functools.partial(body, n_ctx=mesh.shape["ctx"], n_tp=mesh.shape["tp"]),
        mesh=mesh,
        in_specs=placed,
        out_specs=(P("tp", "ctx"), P("tp", "ctx"), P("tp", "ctx"), P("ctx", "tp")),
        check_vma=False,
    )
```
